256 devices in a mesh: grp: 8 (over z), leaf: 32 (over y, x, core).
Axes of the slice: x: 4, y: 4, z: 8, core: 2. Of those that a mesh axis runs over, the one named last changes fastest.
Arguments:
- configs: bfloat16 [524288, 64], P(('grp', 'leaf')), may hold values from -6 to 6, as said below
- order: int32 [256, 2048], P(('grp', 'leaf')), may hold values from 0 to 2047, each once within a row
- w_in: bfloat16 [64, 128], replicated, may hold values from -0.75 to 0.75
- bias_in: float32 [128], replicated, may hold values from -3 to 3
- w_out: bfloat16 [128, 128], replicated, may hold values from -0.5 to 0.5
- noise: float32 [524288], P(('grp', 'leaf')), may hold values from 0.2 to 2
- right_side: float32 [524288], P(('grp', 'leaf')), may hold values from -12 to 12, as said below
- near_blocks: int32 [2048, 6], P(('grp', 'leaf')), may hold values from 0 to 255
- near_live: int32 [2048, 6], P(('grp', 'leaf')), may hold values 0 or 1
- skeleton: int32 [8, 256], P('grp'), may hold values from 0 to 65535
Outputs:
- solution: float32 [524288], P(('grp', 'leaf'))
- residual: float32 [524288], P(('grp', 'leaf'))
The draws below stay inside these ranges and needn't reach their ends.
Inputs may be any that keep to these rules, and one draw needn't show every extreme that they name: `configs`: configurations of order one. `right_side`: targets of order one.
All inputs are finite; a program needn't handle non-finite values. No bound on the sum of `near_live` on one device may be relied on, other than what follows from the above.
Results may differ from the reference program's by a relative error of at most 0.039.
Values may be sent and summed in bfloat16 or wider, within the bound.
A program may use at most 128 MiB of HBM per device.

```python
import math
import jax
import jax.numpy as jnp
from jax import lax

ROWS_DEV = 2048
DIN = 64
HID = 128
FEAT = 128
RANK = 256
BLK = 256
NEAR = 6
ITERS = 4
GROUP_ROWS = 65536
GROUP_BLOCKS = 256
ROWS = 524288
BLOCKS = 2048
N_GRP = 8
N_LEAF = 32


def draw_configs(key, part):
    key_cluster, key_centre, key_tightness, key_row = jax.random.split(key, 4)
    clusters = max(ROWS // 512, 8)
    member = jax.random.randint(key_cluster, (ROWS,), 0, clusters)
    centre = jnp.clip(jax.random.normal(key_centre, (clusters, DIN), jnp.float32), -4.0, 4.0)
    tightness = jax.random.uniform(key_tightness, (ROWS, 1), jnp.float32, 0.15, 0.4)
    spread = jnp.clip(jax.random.normal(key_row, (ROWS, DIN), jnp.float32), -4.0, 4.0)
    values = jnp.take(centre, member, axis=0) + tightness * spread
    return values.astype(jnp.bfloat16)


def draw_right_side(key, part):
    position = jnp.arange(ROWS, dtype=jnp.float32) / (ROWS - 1)
    rising = 1.0 + 2.0 * position
    values = jnp.clip(jax.random.normal(key, (ROWS,), jnp.float32), -4.0, 4.0)
    return values * rising


def set_ends(values, stream_key, smallest, top_value):
    longest = values.shape.index(max(values.shape))
    spots = []
    for shift in (0, 1):
        where = [jax.random.randint(jax.random.fold_in(stream_key, axis), (), 0, length) for axis, length in enumerate(values.shape)]
        where[longest] = (where[longest] + shift) % values.shape[longest]
        spots.append(tuple(where))
    return values.at[spots[0]].set(smallest).at[spots[1]].set(top_value)


def block_scale(own_key, shape, cuts, low, high):
    def one(axis_at, blocks):
        heights = jax.random.uniform(jax.random.fold_in(jax.random.fold_in(own_key, 6), axis_at), (blocks,), jnp.float32, low / len(cuts), high / len(cuts))
        return jnp.repeat(jnp.exp(heights), shape[axis_at] // blocks).reshape((-1,) + (1,) * (len(shape) - axis_at - 1))

    level = one(*cuts[0])
    for cut in cuts[1:]:
        level = level * one(*cut)
    return level


def scatter_about(key, dims, width, limit, held_as=jnp.bfloat16):
    drawn = jax.random.normal(key, dims, jnp.float32) * width
    return jnp.minimum(jnp.maximum(drawn, -limit), limit).astype(held_as)


def setup_inputs(seed: int = 0) -> dict:
    arg_keys = jax.random.split(jax.random.key(seed), 11)
    return {
        "configs": draw_configs(jax.random.fold_in(arg_keys[10], 71), 0),
        "order": jax.vmap(lambda own: jax.random.permutation(own, ROWS_DEV))(jax.random.split(arg_keys[1], (N_GRP * N_LEAF))).reshape((N_GRP * N_LEAF, ROWS_DEV)).astype(jnp.int32),
        "w_in": scatter_about(arg_keys[2], (DIN, HID), DIN ** -0.5, 0.75),
        "bias_in": scatter_about(arg_keys[3], (HID,), 0.5, 3.0, jnp.float32),
        "w_out": scatter_about(arg_keys[4], (HID, FEAT), HID ** -0.5, 0.5),
        "noise": jnp.clip(jnp.exp(math.log(2.0) - 2.3025851 * jax.random.uniform(arg_keys[5], (ROWS,), jnp.float32) ** block_scale(arg_keys[5], (ROWS,), ((0, 256),), -0.2, 0.2)), 0.2, 2.0),
        "right_side": draw_right_side(jax.random.fold_in(arg_keys[10], 71), 0),
        "near_blocks": set_ends(jax.random.randint(arg_keys[7], (BLOCKS, NEAR), 0, GROUP_BLOCKS), jax.random.fold_in(arg_keys[7], 1), 0, GROUP_BLOCKS - 1).astype(jnp.int32),
        "near_live": set_ends((jax.random.randint(arg_keys[8], (BLOCKS, NEAR), 0, 4) < 3).astype(jnp.int32), jax.random.fold_in(arg_keys[8], 1), 0, 1),
        "skeleton": set_ends(jax.random.randint(arg_keys[9], (N_GRP, RANK), 0, GROUP_ROWS), jax.random.fold_in(arg_keys[9], 1), 0, GROUP_ROWS - 1).astype(jnp.int32),
    }


sharpness = 10.0
highest = lax.Precision.HIGHEST

def kernel_rows(left, right):
    inner = jnp.einsum('if,jf->ij', left.astype(jnp.float32), right.astype(jnp.float32), precision=highest)
    return jnp.exp(sharpness * (inner - 1.0))

def features_of(inputs, w_in, bias_in, w_out):
    hidden = jnp.tanh(jnp.dot(inputs, w_in, preferred_element_type=jnp.float32) + bias_in).astype(jnp.bfloat16)
    raw = jnp.dot(hidden, w_out, preferred_element_type=jnp.float32)
    return (raw * lax.rsqrt(lax.optimization_barrier(jnp.sum(raw * raw, -1, keepdims=True)) + 1e-06)).astype(jnp.bfloat16)

def reference(configs, order, w_in, bias_in, w_out, noise, right_side, near_blocks, near_live, skeleton):
    grouped = configs.reshape(N_GRP * N_LEAF, ROWS_DEV, DIN)
    tree_rows = jax.vmap(lambda rows_in, perm: jnp.take(rows_in, perm, axis=0))(grouped, order).reshape(ROWS, DIN)
    features = features_of(tree_rows, w_in, bias_in, w_out)
    group_feat = features.reshape(N_GRP, GROUP_ROWS, FEAT)
    skel_feat = jax.vmap(lambda feats, picks: jnp.take(feats, picks, axis=0))(group_feat, skeleton)
    skel_flat = skel_feat.reshape(N_GRP * RANK, FEAT)
    coupling = kernel_rows(skel_flat, skel_flat)
    block_feat = group_feat.reshape(N_GRP, GROUP_BLOCKS, BLK, FEAT)
    live_mask = near_live.astype(jnp.float32)
    total_blocks = N_GRP * GROUP_BLOCKS

    def near(vector):
        vec_blocks = vector.reshape(N_GRP, GROUP_BLOCKS, BLK)

        def one_block(index):
            group_id = index // GROUP_BLOCKS
            block_id = index % GROUP_BLOCKS
            own_feat = block_feat[group_id, block_id]
            partners = near_blocks[index]
            weights = live_mask[index]
            part_feat = jnp.take(block_feat[group_id], partners, axis=0).astype(jnp.float32)
            own_vec = vec_blocks[group_id, block_id]
            part_vec = jnp.take(vec_blocks[group_id], partners, axis=0)
            self_tile = kernel_rows(own_feat, own_feat)
            cross = jnp.exp(sharpness * (jnp.einsum('if,kjf->kij', own_feat.astype(jnp.float32), part_feat, precision=highest) - 1.0))
            partner_tile = jnp.exp(sharpness * (jnp.einsum('kif,kjf->kij', part_feat, part_feat, precision=highest) - 1.0))
            own_out = jnp.sum(weights) * jnp.dot(self_tile, own_vec, precision=highest)
            own_out = own_out + lax.optimization_barrier(jnp.sum(weights[:, None] * jnp.einsum('kij,kj->ki', cross, part_vec, precision=highest), 0))
            back = jnp.einsum('kij,i->kj', cross, own_vec, precision=highest) + jnp.einsum('kij,kj->ki', partner_tile, part_vec, precision=highest)
            return (own_out, weights[:, None] * back)
        own_all, back_all = lax.map(one_block, jnp.arange(total_blocks, dtype=jnp.int32))
        target = (jnp.arange(total_blocks, dtype=jnp.int32) // GROUP_BLOCKS)[:, None] * GROUP_BLOCKS + near_blocks
        result = own_all.at[target.reshape(-1)].add(back_all.reshape(-1, BLK))
        return result.reshape(-1)

    def far(vector):
        vec_groups = vector.reshape(N_GRP, GROUP_ROWS)

        def charge(group_id):
            basis = kernel_rows(group_feat[group_id], skel_feat[group_id])
            return jnp.dot(vec_groups[group_id], basis, precision=highest)
        charges = lax.map(charge, jnp.arange(N_GRP, dtype=jnp.int32))
        field = jnp.dot(coupling, charges.reshape(-1), precision=highest).reshape(N_GRP, RANK)

        def spread(group_id):
            basis = kernel_rows(group_feat[group_id], skel_feat[group_id])
            return jnp.dot(basis, field[group_id], precision=highest)
        return lax.map(spread, jnp.arange(N_GRP, dtype=jnp.int32)).reshape(-1)

    def apply(vector):
        return near(vector) + far(vector) + noise * vector
    precond = 1.0 / (1.0 + noise)
    solution = jnp.zeros_like(right_side)
    residual = right_side
    scaled = residual * precond
    direction = scaled
    product_now = jnp.sum(residual * scaled)
    for step in range(ITERS):
        image = apply(direction)
        step_size = product_now / jnp.sum(direction * image)
        solution = solution + step_size * direction
        residual = residual - step_size * image
        if step + 1 < ITERS:
            scaled = residual * precond
            product_next = jnp.sum(residual * scaled)
            direction = scaled + product_next / product_now * direction
            product_now = product_next
    return (solution, residual)
```

```python
import jax
import jax.numpy as jnp
from jax import lax
from jax.experimental import pallas as pl
from jax.experimental.pallas import tpu as pltpu
from jax.sharding import PartitionSpec as P

BLK = 256
NEAR = 6
ITERS = 4
N_GRP = 8
N_LEAF = 32
OWN = 8
ROWS_DEV = OWN * BLK
HALF = BLK // 2
F32 = jnp.float32
BF16 = jnp.bfloat16
MESH = pl.DeviceIdType.MESH
SHARP = 10.0 * 1.4426950408889634


def mm(left, right):
    return lax.dot_general(left, right, (((1,), (0,)), ((), ())), preferred_element_type=F32)


def mm_t(left, right):
    return lax.dot_general(left, right, (((1,), (1,)), ((), ())), preferred_element_type=F32)


def iota(shape, dim):
    return lax.broadcasted_iota(jnp.int32, shape, dim)


def kernel_of(inner):
    return jnp.exp2(inner * SHARP - SHARP)


def unit(raw):
    return (raw * lax.rsqrt(jnp.sum(raw * raw, -1, keepdims=True) + 1e-06)).astype(BF16)


def split2(values):
    high = values.astype(BF16).astype(F32)
    return high, (values - high).astype(BF16).astype(F32)


def rows16(values):
    return jnp.concatenate(split2(values), 0).astype(BF16)


def spread(values):
    wide = jnp.concatenate([jnp.concatenate(split2(values), 0)] * OWN, 1)
    shape = (16, ROWS_DEV)
    keep = (iota(shape, 0) & 7) == (iota(shape, 1) >> 8)
    return jnp.where(keep, wide, 0.0).astype(BF16)


def own_part(wide):
    both = wide[:8] + wide[8:]
    row = iota((8, BLK), 0)
    total = jnp.zeros((8, BLK), F32)
    for n in range(OWN):
        total = total + jnp.where(row == n, both[:, n * BLK : (n + 1) * BLK], 0.0)
    return total


def halves(values):
    return jnp.concatenate([values[:8], values[8:]], 1)


def sum_all(values):
    folded = values[:, :128] + values[:, 128:]
    return jnp.broadcast_to(jnp.sum(folded, (0, 1), keepdims=True), (8, 128))


def wide(values):
    return jnp.concatenate([values, values], 1)


def column_of(row):
    return jnp.transpose(jnp.broadcast_to(row.astype(F32), (128, 128)))


def body(
    cfg_ref, order_ref, w_in_ref, bias_ref, w_out_ref, noise_ref, rhs_ref, nb_ref, live_ref, skel_ref,
    nb_s, skel_s,
    x_out, r_out,
    grp_cfg, tiles, coup, skel_all, slabs, pick, pick_t,
    msg_a, ret_send, ret_recv, quad, grp_q, grp_s,
    g_send, g_recv, s_send, s_recv, k_sem, it_sem,
):
    grp = lax.axis_index("grp")
    me = lax.axis_index("leaf")
    core = lax.rem(me, 2)
    xx = lax.rem(me // 2, 4)
    yy = me // 8

    def leaf_at(y, x, c):
        return lax.rem(y + 4, 4) * 8 + lax.rem(x + 4, 4) * 2 + c

    def leaf_peer(j):
        return lax.rem(me + j, N_LEAF)

    def grp_peer(j):
        return lax.rem(grp + j, N_GRP)

    barrier = pltpu.get_barrier_semaphore()

    def greet_leaf(j, _):
        pl.semaphore_signal(barrier, inc=1, device_id=(grp, leaf_peer(j)), device_id_type=MESH)
        return 0

    def greet_grp(j, _):
        pl.semaphore_signal(barrier, inc=1, device_id=(grp_peer(j), me), device_id_type=MESH)
        return 0

    lax.fori_loop(1, N_LEAF, greet_leaf, 0)
    lax.fori_loop(1, N_GRP, greet_grp, 0)

    spot0 = (iota((64, 128), 0) == iota((64, 128), 1)).astype(F32).astype(BF16)
    spot1 = (iota((64, 128), 0) + 64 == iota((64, 128), 1)).astype(F32).astype(BF16)
    lane = iota((128, 128), 1).astype(F32)

    def permute(b, _):
        packed = jnp.zeros((HALF, 128), F32)
        for half, spot in ((0, spot0), (1, spot1)):
            column = column_of(order_ref[pl.ds(2 * b + half, 1), :])
            chosen = jnp.concatenate(
                [jnp.where(column == lane + 128.0 * t, 1.0, 0.0).astype(BF16) for t in range(ROWS_DEV // 128)], 1
            )
            packed = packed + mm(mm(chosen, cfg_ref[...]).astype(BF16), spot)
        grp_cfg[me * OWN + b] = packed.astype(BF16)
        return 0

    lax.fori_loop(0, OWN, permute, 0)
    pl.semaphore_wait(barrier, N_LEAF - 1 + N_GRP - 1)

    def at(half, first, second):
        return leaf_at(yy + second, xx + first, core) if half == 0 else leaf_at(yy + first, xx + second, core)

    def piece(leaf, half, quarter=None):
        if quarter is None:
            return grp_cfg.at[pl.ds(leaf * OWN + 4 * half, 4)]
        return grp_cfg.at[pl.ds(leaf * OWN + 4 * half + 2 * quarter, 2)]

    def hop(half, index, ref, target):
        return pltpu.make_async_remote_copy(
            src_ref=ref, dst_ref=ref, send_sem=g_send.at[half, index], recv_sem=g_recv.at[half, index],
            device_id=(grp, target), device_id_type=MESH,
        )

    sibling = me - core + lax.rem(core + 1, 2)

    def to_sibling(half, index, leaf):
        ref = piece(leaf, half)
        copy = pltpu.make_async_remote_copy(
            src_ref=ref, dst_ref=ref, send_sem=s_send.at[half, index], recv_sem=s_recv.at[half, index],
            device_id=(grp, sibling), device_id_type=MESH,
        )
        copy.start()
        return copy

    started = []

    def start(copy):
        copy.start()
        started.append(copy)

    offsets = (0, -1, 1, 2)

    def second_axis(half, p):
        ref = piece(at(half, offsets[p], 0), half)
        start(hop(half, 4 + 4 * p, ref, at(half, 0, 1)))
        start(hop(half, 5 + 4 * p, ref, at(half, 0, -1)))
        started.append(to_sibling(half, 4 * p, at(half, offsets[p], 0)))

    def arrived(half, index, ref):
        hop(half, index, ref, me).wait_recv()

    for half in range(2):
        own = piece(me, half)
        start(hop(half, 0, own, at(half, 1, 0)))
        start(hop(half, 1, own, at(half, -1, 0)))
    for half in range(2):
        second_axis(half, 0)
    for half in range(2):
        left, right = at(half, -1, 0), at(half, 1, 0)
        arrived(half, 0, piece(left, half))
        start(hop(half, 2, piece(left, half, 0), right))
        arrived(half, 1, piece(right, half))
        start(hop(half, 3, piece(right, half, 1), left))
    for half in range(2):
        second_axis(half, 1)
        second_axis(half, 2)
    for p in range(4):
        for half in range(2):
            if p == 1:
                far = at(half, 2, 0)
                arrived(half, 2, piece(far, half, 0))
                arrived(half, 3, piece(far, half, 1))
                second_axis(half, 3)
        for half in range(2):
            down, up = at(half, offsets[p], -1), at(half, offsets[p], 1)
            arrived(half, 4 + 4 * p, piece(down, half))
            start(hop(half, 6 + 4 * p, piece(down, half, 0), at(half, 0, 1)))
            started.append(to_sibling(half, 4 * p + 1, down))
            arrived(half, 5 + 4 * p, piece(up, half))
            start(hop(half, 7 + 4 * p, piece(up, half, 1), at(half, 0, -1)))
            started.append(to_sibling(half, 4 * p + 2, up))
        for half in range(2):
            over = at(half, offsets[p], 2)
            arrived(half, 6 + 4 * p, piece(over, half, 0))
            arrived(half, 7 + 4 * p, piece(over, half, 1))
            started.append(to_sibling(half, 4 * p + 3, over))
    steps = (0, -1, 1, 2)
    for p in range(4):
        for half in range(2):
            for s in range(4):
                theirs = at(half, offsets[p], steps[s]) - core + lax.rem(core + 1, 2)
                ref = piece(theirs, half)
                pltpu.make_async_remote_copy(
                    src_ref=ref, dst_ref=ref, send_sem=s_send.at[half, 4 * p + s], recv_sem=s_recv.at[half, 4 * p + s],
                    device_id=(grp, sibling), device_id_type=MESH,
                ).wait_recv()
    for copy in started:
        copy.wait_send()

    w_in = w_in_ref[...]
    none = jnp.zeros_like(w_in)
    w_pair = jnp.concatenate([jnp.concatenate([w_in, none], 1), jnp.concatenate([none, w_in], 1)], 0)
    bias = jnp.concatenate([bias_ref[...], bias_ref[...]], 1)
    w_out = w_out_ref[...]

    def hidden_of(packed):
        return jnp.tanh(mm(packed, w_pair) + bias)

    def slab(r, _):
        block = grp_cfg[skel_s[0, r]].astype(F32)
        kept = jnp.where(iota((HALF, 128), 0) >> 4 == jnp.broadcast_to(skel_s[1, r], (HALF, 128)), block, 0.0)
        slabs[r] = jnp.sum(kept.reshape(8, 16, 128), 0).astype(BF16)
        return 0

    lax.fori_loop(0, BLK, slab, 0)
    every = slabs[...].reshape(BLK * 16, 128)
    for part in range(2):
        column = jnp.transpose(jnp.broadcast_to(skel_ref[pl.ds(part, 1), :], (128, 128)).astype(F32)).astype(jnp.int32)
        aim = (column & 15) + 16 * iota((128, 128), 0)
        chosen = jnp.concatenate(
            [jnp.where(aim == iota((128, 128), 1) + 128 * t, 1.0, 0.0).astype(BF16) for t in range(16)], 1
        )
        packed = mm(chosen, every[part * 2048 : (part + 1) * 2048]).astype(BF16)
        hidden = hidden_of(packed)
        hidden = jnp.where((column & HALF) != 0, hidden[:, 128:], hidden[:, :128]).astype(BF16)
        skel_all[grp, pl.ds(part * 128, 128), :] = unit(mm(hidden, w_out))

    def skel_copy(j):
        return pltpu.make_async_remote_copy(
            src_ref=skel_all.at[grp], dst_ref=skel_all.at[grp], send_sem=k_sem.at[0], recv_sem=k_sem.at[1],
            device_id=(grp_peer(j), me), device_id_type=MESH,
        )

    def start_skel(j, _):
        skel_copy(j).start()
        return 0

    lax.fori_loop(1, N_GRP, start_skel, 0)

    skel_feat = skel_all[grp]

    def tile_row(n, _):
        packed = jnp.concatenate(
            [grp_cfg[nb_s[n, k]] for k in range(NEAR)] + [grp_cfg[me * OWN + n]], 0
        )
        hidden = hidden_of(packed).astype(BF16)
        feats = [unit(mm(hidden[:, :128], w_out)), unit(mm(hidden[:, 128:], w_out))]
        own = jnp.concatenate([f[NEAR * HALF :] for f in feats], 0)
        rows = pl.ds(n * BLK, BLK)
        for h in range(2):
            made = kernel_of(mm_t(own, feats[h])).astype(BF16)
            for k in range(NEAR):
                tiles[k, rows, h * 128 : (h + 1) * 128] = made[:, k * 128 : (k + 1) * 128]
            tiles[NEAR + 1, rows, h * 128 : (h + 1) * 128] = made[:, NEAR * 128 :]
        tiles[NEAR, rows, :] = kernel_of(mm_t(own, skel_feat)).astype(BF16)
        return 0

    lax.fori_loop(0, OWN, tile_row, 0)

    nb = nb_ref[...]
    live = live_ref[...].astype(F32)
    place = nb + (nb & -8)
    for h in range(2):
        for k in range(NEAR):
            hit = iota((8, 512), 1) == place[:, k : k + 1] + 8 * h
            pick[pl.ds((h * NEAR + k) * 8, 8), :] = jnp.where(hit, live[:, k : k + 1], 0.0)
    pick[pl.ds(96, 32), :] = jnp.zeros((32, 512), F32)
    for q in range(4):
        pick_t[pl.ds(q * 128, 128), :] = jnp.transpose(pick[:, q * 128 : (q + 1) * 128]).astype(BF16)
    count = jnp.zeros((8, BLK), F32)
    for k in range(NEAR):
        count = count + jnp.where(iota((8, BLK), 1) == nb[:, k : k + 1], live[:, k : k + 1], 0.0)
    count = jnp.sum(count, 0, keepdims=True)
    own_uses = jnp.sum(live, 1, keepdims=True)

    many = skel_all.at[pl.ds(0, N_GRP - 1)]
    pltpu.make_async_copy(many, many, k_sem.at[1]).wait()
    pltpu.make_async_copy(many, many, k_sem.at[0]).wait()

    def couple(g, _):
        coup[pl.ds(g * BLK, BLK), :] = kernel_of(mm_t(skel_all[g], skel_feat)).astype(BF16)
        return 0

    lax.fori_loop(0, N_GRP, couple, 0)

    noise = jnp.concatenate([noise_ref[pl.ds(0, 8, stride=2), :], noise_ref[pl.ds(1, 8, stride=2), :]], 1)
    right = jnp.concatenate([rhs_ref[pl.ds(0, 8, stride=2), :], rhs_ref[pl.ds(1, 8, stride=2), :]], 1)
    precond = 1.0 / (1.0 + noise)
    zero = jnp.zeros((8, BLK), F32)
    one = jnp.ones((8, 128), F32)

    def iteration(t, carry):
        x, r, direction, image, gamma_old, energy_old = carry
        sem = it_sem.at[t]
        u = r * precond
        gamma_own = sum_all(r * u)
        mixed_own = sum_all(u * image)
        u_wide = spread(u)
        charge = jnp.sum(mm(u_wide, tiles[NEAR]), 0, keepdims=True)

        c_high, c_mid = split2(charge)
        g_high, g_mid = split2(gamma_own)
        g_low = gamma_own - g_high - g_mid
        m_high, m_mid = split2(mixed_own)
        m_low = mixed_own - m_high - m_mid
        row = iota((16, 128), 0)
        extra = jnp.zeros((16, 128), F32)
        for at_row, values in enumerate(
            (c_high[:, :128], c_high[:, 128:], c_mid[:, :128], c_mid[:, 128:], count[:, :128], count[:, 128:],
             g_high[:1], g_mid[:1], g_low[:1], m_high[:1], m_mid[:1], m_low[:1])
        ):
            extra = jnp.where(row == at_row, values, extra)
        msg_a[t, me, pl.ds(0, 16), :] = jnp.concatenate([u[:, :128], u[:, 128:]], 0).astype(BF16)
        msg_a[t, me, pl.ds(16, 16), :] = extra.astype(BF16)

        def send_a(j, _):
            pltpu.make_async_remote_copy(
                src_ref=msg_a.at[t, me], dst_ref=msg_a.at[t, me], send_sem=sem.at[0], recv_sem=sem.at[1],
                device_id=(grp, leaf_peer(j)), device_id_type=MESH,
            ).start()
            return 0

        lax.fori_loop(1, N_LEAF, send_a, 0)

        backs = []
        for k in range(NEAR):
            made = mm(u_wide, tiles[k])
            backs.append(made[:8] + made[8:])
        stack = jnp.concatenate([b[:, :128] for b in backs] + [b[:, 128:] for b in backs] + [jnp.zeros((32, 128), F32)], 0)
        b_high, b_mid = split2(stack)
        returned = mm(pick_t[...], b_high.astype(BF16)) + mm(pick_t[...], b_mid.astype(BF16))
        ret_send[t] = returned.reshape(N_LEAF, 16, 128).astype(BF16)
        ret_recv[t, me] = ret_send[t, me]

        def send_r(j, _):
            peer = leaf_peer(j)
            pltpu.make_async_remote_copy(
                src_ref=ret_send.at[t, peer], dst_ref=ret_recv.at[t, me], send_sem=sem.at[2], recv_sem=sem.at[3],
                device_id=(grp, peer), device_id_type=MESH,
            ).start()
            return 0

        lax.fori_loop(1, N_LEAF, send_r, 0)
        made = mm(u_wide, tiles[NEAR + 1])
        self_part = made[:8] + made[8:]

        many = msg_a.at[t, pl.ds(0, N_LEAF - 1)]
        pltpu.make_async_copy(many, many, sem.at[1]).wait()
        extra = jnp.sum(msg_a[t, :, pl.ds(16, 16), :].astype(F32), 0)
        charge = jnp.concatenate([extra[0:1] + extra[2:3], extra[1:2] + extra[3:4]], 1)
        counts = jnp.broadcast_to(jnp.concatenate([extra[4:5], extra[5:6]], 1), (8, BLK))
        mine = iota((8, BLK), 1) == me * OWN + iota((8, BLK), 0)
        weight = own_uses + jnp.sum(jnp.where(mine, counts, 0.0), 1, keepdims=True)
        self_part = weight * self_part
        row = iota((8, 128), 0)
        tile = jnp.where(row == 0, charge[:, :128], 0.0)
        tile = jnp.where(row == 1, charge[:, 128:], tile)
        tile = jnp.where(row == 2, extra[6:7] + extra[7:8] + extra[8:9], tile)
        tile = jnp.where(row == 3, extra[9:10] + extra[10:11] + extra[11:12], tile)
        grp_q[t, grp] = tile

        def send_q(j, _):
            pltpu.make_async_remote_copy(
                src_ref=grp_q.at[t, grp], dst_ref=grp_q.at[t, grp], send_sem=sem.at[4], recv_sem=sem.at[5],
                device_id=(grp_peer(j), me), device_id_type=MESH,
            ).start()
            return 0

        lax.fori_loop(1, N_GRP, send_q, 0)

        vectors = msg_a[t, :, pl.ds(0, 16), :].reshape(N_LEAF * 16, 128)
        found = mm(pick[...].astype(BF16), vectors)
        partners = [
            jnp.concatenate([found[k * 8 : k * 8 + 8], found[(NEAR + k) * 8 : (NEAR + k) * 8 + 8]], 1) for k in range(NEAR)
        ]
        share = u * (self_part + noise * u)
        for k in range(NEAR):
            share = share + 2.0 * backs[k] * partners[k]
        quad[t, me] = sum_all(share)[:1]

        def send_s(j, _):
            pltpu.make_async_remote_copy(
                src_ref=quad.at[t, me], dst_ref=quad.at[t, me], send_sem=sem.at[6], recv_sem=sem.at[7],
                device_id=(grp, leaf_peer(j)), device_id_type=MESH,
            ).start()
            return 0

        lax.fori_loop(1, N_LEAF, send_s, 0)

        forward = jnp.zeros((16, ROWS_DEV), F32)
        for k in range(NEAR):
            forward = forward + mm_t(jnp.concatenate([partners[k], zero], 0).astype(BF16), tiles[k])
        near = self_part + own_part(forward)

        many = grp_q.at[t, pl.ds(0, N_GRP - 1)]
        pltpu.make_async_copy(many, many, sem.at[5]).wait()
        row = iota((8, BLK), 0)
        charges = zero
        sums = jnp.zeros((8, 128), F32)
        for g in range(N_GRP):
            tile = grp_q[t, g]
            charges = jnp.where(row == g, jnp.concatenate([tile[0:1], tile[1:2]], 1), charges)
            sums = sums + tile
        gamma = jnp.broadcast_to(sums[2:3], (8, 128))
        mixed = jnp.broadcast_to(sums[3:4], (8, 128))
        field = jnp.sum(mm(spread(charges), coup[...]), 0, keepdims=True)
        far_share = sum_all(jnp.where(row == 0, charge * field, 0.0))
        many = quad.at[t, pl.ds(0, N_LEAF - 1)]
        pltpu.make_async_copy(many, many, sem.at[7]).wait()
        grp_s[t, grp] = jnp.sum(quad[t], 0) + far_share[:1]

        def send_c(j, _):
            pltpu.make_async_remote_copy(
                src_ref=grp_s.at[t, grp], dst_ref=grp_s.at[t, grp], send_sem=sem.at[8], recv_sem=sem.at[9],
                device_id=(grp_peer(j), me), device_id_type=MESH,
            ).start()
            return 0

        lax.fori_loop(1, N_GRP, send_c, 0)
        far = own_part(mm_t(rows16(jnp.broadcast_to(field, (8, BLK))), tiles[NEAR]))
        many = ret_recv.at[t, pl.ds(0, N_LEAF - 1)]
        pltpu.make_async_copy(many, many, sem.at[3]).wait()
        near = near + halves(jnp.sum(ret_recv[t].astype(F32), 0))
        applied = near + far + noise * u

        many = grp_s.at[t, pl.ds(0, N_GRP - 1)]
        pltpu.make_async_copy(many, many, sem.at[9]).wait()
        quadratic = jnp.broadcast_to(jnp.sum(grp_s[t], 0), (8, 128))
        beta = jnp.where(t == 0, jnp.zeros_like(gamma), gamma / gamma_old)
        energy = quadratic + 2.0 * beta * mixed + beta * beta * energy_old
        alpha = wide(gamma / energy)
        direction = u + wide(beta) * direction
        image = applied + wide(beta) * image
        x = x + alpha * direction
        r = r - alpha * image

        for index, sent in (
            (0, msg_a.at[t, pl.ds(0, N_LEAF - 1)]),
            (2, ret_recv.at[t, pl.ds(0, N_LEAF - 1)]),
            (4, grp_q.at[t, pl.ds(0, N_GRP - 1)]),
            (6, quad.at[t, pl.ds(0, N_LEAF - 1)]),
            (8, grp_s.at[t, pl.ds(0, N_GRP - 1)]),
        ):
            pltpu.make_async_copy(sent, sent, sem.at[index]).wait()
        return x, r, direction, image, gamma, energy

    x, r, *_ = lax.fori_loop(0, ITERS, iteration, (zero, right, zero, zero, one, one))
    for ref, values in ((x_out, x), (r_out, r)):
        ref[pl.ds(0, 8, stride=2), :] = values[:, :128]
        ref[pl.ds(1, 8, stride=2), :] = values[:, 128:]


def on_device(
    configs, order, w_in, bias_in, w_out, noise, right_side, near_blocks, near_live, skeleton
):
    vmem = pl.BlockSpec(memory_space=pltpu.VMEM)
    smem = pl.BlockSpec(memory_space=pltpu.SMEM)
    dma = pltpu.SemaphoreType.DMA
    solution_, residual_ = pl.pallas_call(
        body,
        out_shape=[jax.ShapeDtypeStruct((16, 128), F32)] * 2,
        in_specs=[vmem] * 10 + [smem] * 2,
        out_specs=[vmem] * 2,
        scratch_shapes=[
            pltpu.VMEM((N_LEAF * OWN, HALF, 128), BF16),
            pltpu.VMEM((NEAR + 2, ROWS_DEV, BLK), BF16),
            pltpu.VMEM((N_GRP * BLK, BLK), BF16),
            pltpu.VMEM((N_GRP, BLK, 128), BF16),
            pltpu.VMEM((BLK, 16, 128), BF16),
            pltpu.VMEM((128, 512), F32),
            pltpu.VMEM((512, 128), BF16),
            pltpu.VMEM((ITERS, N_LEAF, 32, 128), BF16),
            pltpu.VMEM((ITERS, N_LEAF, 16, 128), BF16),
            pltpu.VMEM((ITERS, N_LEAF, 16, 128), BF16),
            pltpu.VMEM((ITERS, N_LEAF, 1, 128), F32),
            pltpu.VMEM((ITERS, N_GRP, 8, 128), F32),
            pltpu.VMEM((ITERS, N_GRP, 1, 128), F32),
            dma((2, 20)),
            dma((2, 20)),
            dma((2, 16)),
            dma((2, 16)),
            dma((2,)),
            dma((ITERS, 10)),
        ],
        compiler_params=pltpu.CompilerParams(
            collective_id=0, has_side_effects=True, vmem_limit_bytes=56 * 2**20
        ),
        cost_estimate=pl.CostEstimate(flops=10**10, bytes_accessed=10**7, transcendentals=10**7),
    )(
        configs, order.reshape(16, 128), w_in, bias_in.reshape(1, 128), w_out,
        noise.reshape(16, 128), right_side.reshape(16, 128), near_blocks, near_live, skeleton.reshape(2, 128),
        near_blocks, jnp.concatenate([skeleton // BLK, skeleton % HALF // 16], 0),
    )
    return solution_.reshape(-1), residual_.reshape(-1)


def solution(mesh):
    in_specs = (
        P(("grp", "leaf"), None),
        P(("grp", "leaf"), None),
        P(),
        P(),
        P(),
        P(("grp", "leaf")),
        P(("grp", "leaf")),
        P(("grp", "leaf"), None),
        P(("grp", "leaf"), None),
        P("grp", None),
    )
    out_specs = (P(("grp", "leaf")), P(("grp", "leaf")))
    return jax.shard_map(
        on_device, mesh=mesh, in_specs=in_specs, out_specs=out_specs, check_vma=False
    )
```

```python
import jax
import jax.numpy as jnp
from jax import lax
from jax.experimental import pallas as pl
from jax.experimental.pallas import tpu as pltpu
from jax.sharding import PartitionSpec as P

BLK = 256
NEAR = 6
ITERS = 4
N_GRP = 8
N_LEAF = 32
OWN = 8
ROWS_DEV = OWN * BLK
F32 = jnp.float32
BF16 = jnp.bfloat16
MESH = pl.DeviceIdType.MESH
SHARP = 10.0 * 1.4426950408889634


def mm(left, right):
    return lax.dot_general(left, right, (((1,), (0,)), ((), ())), preferred_element_type=F32)


def mm_t(left, right):
    return lax.dot_general(left, right, (((1,), (1,)), ((), ())), preferred_element_type=F32)


def iota(shape, dim):
    return lax.broadcasted_iota(jnp.int32, shape, dim)


def kernel_of(inner):
    return jnp.exp2(inner * SHARP - SHARP)


def one_hot(row, base):
    hit = jnp.broadcast_to(row, (BLK, BLK)) == iota((BLK, BLK), 0) + base
    return jnp.where(hit, 1.0, 0.0).astype(BF16)


def flip(values):
    return jnp.transpose(values.astype(F32)).astype(BF16)


def split2(values):
    high = values.astype(BF16).astype(F32)
    return high, (values - high).astype(BF16).astype(F32)


def rows16(values):
    return jnp.concatenate(split2(values), 0).astype(BF16)


def spread(values):
    wide = jnp.concatenate([jnp.concatenate(split2(values), 0)] * OWN, 1)
    shape = (16, ROWS_DEV)
    keep = (iota(shape, 0) & 7) == (iota(shape, 1) >> 8)
    return jnp.where(keep, wide, 0.0).astype(BF16)


def own_part(wide):
    both = wide[:8] + wide[8:]
    row = iota((8, BLK), 0)
    total = jnp.zeros((8, BLK), F32)
    for n in range(OWN):
        total = total + jnp.where(row == n, both[:, n * BLK : (n + 1) * BLK], 0.0)
    return total


def halves(values):
    return jnp.concatenate([values[:8], values[8:]], 1)


def sum_all(values):
    folded = values[:, :128] + values[:, 128:]
    return jnp.broadcast_to(jnp.sum(folded, (0, 1), keepdims=True), (8, 128))


def wide(values):
    return jnp.concatenate([values, values], 1)


def column_of(row):
    return jnp.transpose(jnp.broadcast_to(row.astype(F32), (128, 128)))


def body(
    cfg_ref, order_ref, w_in_ref, bias_ref, w_out_ref, noise_ref, rhs_ref, nb_ref, live_ref, skel_ref,
    nb_s,
    x_out, r_out,
    grp_cfg, tiles, coup, own_feat, part_send, part_recv, skel_tiles, skel_cfg, pick, pick_t,
    msg_a, ret_send, ret_recv, quad, grp_q, grp_s,
    g_send, g_recv, s_send, s_recv, k_sem, it_sem,
):
    grp = lax.axis_index("grp")
    me = lax.axis_index("leaf")
    core = lax.rem(me, 2)
    xx = lax.rem(me // 2, 4)
    yy = me // 8

    def leaf_at(y, x, c):
        return lax.rem(y + 4, 4) * 8 + lax.rem(x + 4, 4) * 2 + c

    def leaf_peer(j):
        return lax.rem(me + j, N_LEAF)

    def grp_peer(j):
        return lax.rem(grp + j, N_GRP)

    barrier = pltpu.get_barrier_semaphore()

    def greet_leaf(j, _):
        pl.semaphore_signal(barrier, inc=1, device_id=(grp, leaf_peer(j)), device_id_type=MESH)
        return 0

    def greet_grp(j, _):
        pl.semaphore_signal(barrier, inc=1, device_id=(grp_peer(j), me), device_id_type=MESH)
        return 0

    lax.fori_loop(1, N_LEAF, greet_leaf, 0)
    lax.fori_loop(1, N_GRP, greet_grp, 0)

    def permute(b, _):
        row = order_ref[:, pl.ds(pl.multiple_of(b * BLK, BLK), BLK)]
        total = jnp.zeros((64, BLK), F32)
        for c in range(OWN):
            total = total + mm(cfg_ref[:, c * BLK : (c + 1) * BLK], one_hot(row, c * BLK))
        grp_cfg[me * OWN + b] = total.astype(BF16)
        return 0

    def at(half, first, second):
        return leaf_at(yy + second, xx + first, core) if half == 0 else leaf_at(yy + first, xx + second, core)

    def piece(leaf, half, quarter=None):
        if quarter is None:
            return grp_cfg.at[pl.ds(leaf * OWN + 4 * half, 4)]
        return grp_cfg.at[pl.ds(leaf * OWN + 4 * half + 2 * quarter, 2)]

    def hop(half, index, ref, target):
        return pltpu.make_async_remote_copy(
            src_ref=ref, dst_ref=ref, send_sem=g_send.at[half, index], recv_sem=g_recv.at[half, index],
            device_id=(grp, target), device_id_type=MESH,
        )

    sibling = me - core + lax.rem(core + 1, 2)

    def to_sibling(half, index, leaf):
        ref = piece(leaf, half)
        copy = pltpu.make_async_remote_copy(
            src_ref=ref, dst_ref=ref, send_sem=s_send.at[half, index], recv_sem=s_recv.at[half, index],
            device_id=(grp, sibling), device_id_type=MESH,
        )
        copy.start()
        return copy

    started = []

    def start(copy):
        copy.start()
        started.append(copy)

    offsets = (0, -1, 1, 2)

    def second_axis(half, p):
        ref = piece(at(half, offsets[p], 0), half)
        start(hop(half, 4 + 4 * p, ref, at(half, 0, 1)))
        start(hop(half, 5 + 4 * p, ref, at(half, 0, -1)))
        started.append(to_sibling(half, 4 * p, at(half, offsets[p], 0)))

    def arrived(half, index, ref):
        hop(half, index, ref, me).wait_recv()

    for half in range(2):
        lax.fori_loop(4 * half, 4 * half + 4, permute, 0)
        if half == 0:
            pl.semaphore_wait(barrier, N_LEAF - 1 + N_GRP - 1)
        own = piece(me, half)
        start(hop(half, 0, own, at(half, 1, 0)))
        start(hop(half, 1, own, at(half, -1, 0)))

    def choose(b, total):
        return total + mm(grp_cfg[me * OWN + b], one_hot(skel_ref[...] - me * ROWS_DEV, b * BLK))

    given = lax.fori_loop(0, OWN, choose, jnp.zeros((64, BLK), F32))
    for q in range(16):
        part_send[q] = given[q // 2 * 8 : q // 2 * 8 + 8, q % 2 * 128 : q % 2 * 128 + 128]
    part_recv[me] = part_send[me // 2]

    def send_part(j, _):
        peer = leaf_peer(j)
        pltpu.make_async_remote_copy(
            src_ref=part_send.at[peer // 2], dst_ref=part_recv.at[me], send_sem=k_sem.at[0], recv_sem=k_sem.at[1],
            device_id=(grp, peer), device_id_type=MESH,
        ).start()
        return 0

    lax.fori_loop(1, N_LEAF, send_part, 0)
    for half in range(2):
        second_axis(half, 0)

    w_in_t = flip(w_in_ref[...])
    w_out_t = flip(w_out_ref[...])
    bias = column_of(bias_ref[...])

    def features(configs):
        hidden = mm(w_in_t, configs)
        hidden = jnp.tanh(hidden + jnp.concatenate([bias] * (configs.shape[1] // 128), 1)).astype(BF16)
        raw = mm(w_out_t, hidden)
        return (raw * lax.rsqrt(jnp.sum(raw * raw, 0, keepdims=True) + 1e-06)).astype(BF16)

    def own_row(n, _):
        feat_t = features(grp_cfg[me * OWN + n])
        feat = flip(feat_t)
        own_feat[n] = feat
        tiles[NEAR + 1, pl.ds(n * BLK, BLK), :] = kernel_of(mm(feat, feat_t)).astype(BF16)
        return 0

    def sum_parts():
        many = part_recv.at[pl.ds(0, N_LEAF - 1)]
        pltpu.make_async_copy(many, many, k_sem.at[1]).wait()
        skel_tiles[me // 2] = jnp.sum(part_recv[...], 0)

        def send_tile(j, _):
            pltpu.make_async_remote_copy(
                src_ref=skel_tiles.at[me // 2], dst_ref=skel_tiles.at[me // 2], send_sem=k_sem.at[2], recv_sem=k_sem.at[3],
                device_id=(grp, leaf_peer(2 * j)), device_id_type=MESH,
            ).start()
            return 0

        lax.fori_loop(1, N_LEAF // 2, send_tile, 0)

    def send_skeleton():
        many = skel_tiles.at[pl.ds(0, N_LEAF // 2 - 1)]
        pltpu.make_async_copy(many, many, k_sem.at[3]).wait()
        for h in range(2):
            skel_cfg[grp, :, h * 128 : (h + 1) * 128] = jnp.concatenate(
                [skel_tiles[2 * q + h] for q in range(8)], 0
            ).astype(BF16)

        def send_skel(j, _):
            pltpu.make_async_remote_copy(
                src_ref=skel_cfg.at[grp], dst_ref=skel_cfg.at[grp], send_sem=k_sem.at[4], recv_sem=k_sem.at[5],
                device_id=(grp_peer(j), me), device_id_type=MESH,
            ).start()
            return 0

        lax.fori_loop(1, N_GRP, send_skel, 0)

    def use_skeletons():
        skel_t = features(skel_cfg[grp])

        def basis(n, _):
            tiles[NEAR, pl.ds(n * BLK, BLK), :] = kernel_of(mm(own_feat[n], skel_t)).astype(BF16)
            return 0

        lax.fori_loop(0, OWN, basis, 0)
        many = skel_cfg.at[pl.ds(0, N_GRP - 1)]
        pltpu.make_async_copy(many, many, k_sem.at[5]).wait()

        def couple(g, _):
            coup[pl.ds(g * BLK, BLK), :] = kernel_of(mm(flip(features(skel_cfg[g])), skel_t)).astype(BF16)
            return 0

        lax.fori_loop(0, N_GRP, couple, 0)

    lax.fori_loop(0, OWN, own_row, 0)
    for half in range(2):
        left, right = at(half, -1, 0), at(half, 1, 0)
        arrived(half, 0, piece(left, half))
        start(hop(half, 2, piece(left, half, 0), right))
        arrived(half, 1, piece(right, half))
        start(hop(half, 3, piece(right, half, 1), left))
    for half in range(2):
        second_axis(half, 1)
        second_axis(half, 2)
    sum_parts()
    for p in range(4):
        if p == 1:
            for half in range(2):
                far = at(half, 2, 0)
                arrived(half, 2, piece(far, half, 0))
                arrived(half, 3, piece(far, half, 1))
                second_axis(half, 3)
            send_skeleton()
        for half in range(2):
            down, up = at(half, offsets[p], -1), at(half, offsets[p], 1)
            arrived(half, 4 + 4 * p, piece(down, half))
            start(hop(half, 6 + 4 * p, piece(down, half, 0), at(half, 0, 1)))
            started.append(to_sibling(half, 4 * p + 1, down))
            arrived(half, 5 + 4 * p, piece(up, half))
            start(hop(half, 7 + 4 * p, piece(up, half, 1), at(half, 0, -1)))
            started.append(to_sibling(half, 4 * p + 2, up))
        if p == 3:
            use_skeletons()
        for half in range(2):
            over = at(half, offsets[p], 2)
            arrived(half, 6 + 4 * p, piece(over, half, 0))
            arrived(half, 7 + 4 * p, piece(over, half, 1))
            started.append(to_sibling(half, 4 * p + 3, over))
    steps = (0, -1, 1, 2)
    for p in range(4):
        for half in range(2):
            for s in range(4):
                theirs = at(half, offsets[p], steps[s]) - core + lax.rem(core + 1, 2)
                ref = piece(theirs, half)
                pltpu.make_async_remote_copy(
                    src_ref=ref, dst_ref=ref, send_sem=s_send.at[half, 4 * p + s], recv_sem=s_recv.at[half, 4 * p + s],
                    device_id=(grp, sibling), device_id_type=MESH,
                ).wait_recv()
    for copy in started:
        copy.wait_send()

    def tile_row(n, _):
        feat_t = features(jnp.concatenate([grp_cfg[nb_s[n, k]] for k in range(NEAR)], 1))
        made = kernel_of(mm(own_feat[n], feat_t)).astype(BF16)
        for k in range(NEAR):
            tiles[k, pl.ds(n * BLK, BLK), :] = made[:, k * BLK : (k + 1) * BLK]
        return 0

    lax.fori_loop(0, OWN, tile_row, 0)

    nb = nb_ref[...]
    live = live_ref[...].astype(F32)
    place = nb + (nb & -8)
    for h in range(2):
        for k in range(NEAR):
            hit = iota((8, 512), 1) == place[:, k : k + 1] + 8 * h
            pick[pl.ds((h * NEAR + k) * 8, 8), :] = jnp.where(hit, live[:, k : k + 1], 0.0)
    pick[pl.ds(96, 32), :] = jnp.zeros((32, 512), F32)
    for q in range(4):
        pick_t[pl.ds(q * 128, 128), :] = jnp.transpose(pick[:, q * 128 : (q + 1) * 128]).astype(BF16)
    count = jnp.zeros((8, BLK), F32)
    for k in range(NEAR):
        count = count + jnp.where(iota((8, BLK), 1) == nb[:, k : k + 1], live[:, k : k + 1], 0.0)
    count = jnp.sum(count, 0, keepdims=True)
    own_uses = jnp.sum(live, 1, keepdims=True)

    for index, sent in (
        (0, part_recv.at[pl.ds(0, N_LEAF - 1)]),
        (2, skel_tiles.at[pl.ds(0, N_LEAF // 2 - 1)]),
        (4, skel_cfg.at[pl.ds(0, N_GRP - 1)]),
    ):
        pltpu.make_async_copy(sent, sent, k_sem.at[index]).wait()

    noise = jnp.concatenate([noise_ref[pl.ds(0, 8, stride=2), :], noise_ref[pl.ds(1, 8, stride=2), :]], 1)
    right = jnp.concatenate([rhs_ref[pl.ds(0, 8, stride=2), :], rhs_ref[pl.ds(1, 8, stride=2), :]], 1)
    precond = 1.0 / (1.0 + noise)
    zero = jnp.zeros((8, BLK), F32)
    one = jnp.ones((8, 128), F32)

    def apply(t, v, dots, last):
        sem = it_sem.at[t]
        v_wide = spread(v)
        charge = jnp.sum(mm(v_wide, tiles[NEAR]), 0, keepdims=True)

        c_high, c_mid = split2(charge)
        rows = [c_high[:, :128], c_high[:, 128:], c_mid[:, :128], c_mid[:, 128:], count[:, :128], count[:, 128:]]
        lane = iota((8, 128), 1)
        sums = jnp.zeros((8, 128), F32)
        for index, values in enumerate(dots):
            sums = jnp.where(lane == index, sum_all(values), sums)
        s_high, s_mid = split2(sums)
        rows += [s_high[:1], s_mid[:1], (sums - s_high - s_mid)[:1]]
        row = iota((16, 128), 0)
        extra = jnp.zeros((16, 128), F32)
        for at_row, values in enumerate(rows):
            extra = jnp.where(row == at_row, values, extra)
        msg_a[t, me, pl.ds(0, 16), :] = jnp.concatenate([v[:, :128], v[:, 128:]], 0).astype(BF16)
        msg_a[t, me, pl.ds(16, 16), :] = extra.astype(BF16)

        def send_a(j, _):
            pltpu.make_async_remote_copy(
                src_ref=msg_a.at[t, me], dst_ref=msg_a.at[t, me], send_sem=sem.at[0], recv_sem=sem.at[1],
                device_id=(grp, leaf_peer(j)), device_id_type=MESH,
            ).start()
            return 0

        lax.fori_loop(1, N_LEAF, send_a, 0)

        backs = []
        for k in range(NEAR):
            made = mm(v_wide, tiles[k])
            backs.append(made[:8] + made[8:])
        stack = jnp.concatenate([b[:, :128] for b in backs] + [b[:, 128:] for b in backs] + [jnp.zeros((32, 128), F32)], 0)
        b_high, b_mid = split2(stack)
        returned = mm(pick_t[...], b_high.astype(BF16)) + mm(pick_t[...], b_mid.astype(BF16))
        ret_send[t] = returned.reshape(N_LEAF, 16, 128).astype(BF16)
        ret_recv[t, me] = ret_send[t, me]

        def send_r(j, _):
            peer = leaf_peer(j)
            pltpu.make_async_remote_copy(
                src_ref=ret_send.at[t, peer], dst_ref=ret_recv.at[t, me], send_sem=sem.at[2], recv_sem=sem.at[3],
                device_id=(grp, peer), device_id_type=MESH,
            ).start()
            return 0

        lax.fori_loop(1, N_LEAF, send_r, 0)
        made = mm(v_wide, tiles[NEAR + 1])
        self_part = made[:8] + made[8:]

        many = msg_a.at[t, pl.ds(0, N_LEAF - 1)]
        pltpu.make_async_copy(many, many, sem.at[1]).wait()
        extra = jnp.sum(msg_a[t, :, pl.ds(16, 16), :].astype(F32), 0)
        charge = jnp.concatenate([extra[0:1] + extra[2:3], extra[1:2] + extra[3:4]], 1)
        row = iota((8, 128), 0)
        tile = jnp.where(row == 0, charge[:, :128], 0.0)
        tile = jnp.where(row == 1, charge[:, 128:], tile)
        tile = jnp.where(row == 2, extra[6:7] + extra[7:8] + extra[8:9], tile)
        grp_q[t, grp] = tile

        def send_q(j, _):
            pltpu.make_async_remote_copy(
                src_ref=grp_q.at[t, grp], dst_ref=grp_q.at[t, grp], send_sem=sem.at[4], recv_sem=sem.at[5],
                device_id=(grp_peer(j), me), device_id_type=MESH,
            ).start()
            return 0

        lax.fori_loop(1, N_GRP, send_q, 0)

        counts = jnp.broadcast_to(jnp.concatenate([extra[4:5], extra[5:6]], 1), (8, BLK))
        mine = iota((8, BLK), 1) == me * OWN + iota((8, BLK), 0)
        weight = own_uses + jnp.sum(jnp.where(mine, counts, 0.0), 1, keepdims=True)
        self_part = weight * self_part
        vectors = msg_a[t, :, pl.ds(0, 16), :].reshape(N_LEAF * 16, 128)
        found = mm(pick[...].astype(BF16), vectors)
        partners = [
            jnp.concatenate([found[k * 8 : k * 8 + 8], found[(NEAR + k) * 8 : (NEAR + k) * 8 + 8]], 1) for k in range(NEAR)
        ]
        if last:
            share = v * (self_part + noise * v)
            for k in range(NEAR):
                share = share + 2.0 * backs[k] * partners[k]
            quad[me] = sum_all(share)[:1]

            def send_s(j, _):
                pltpu.make_async_remote_copy(
                    src_ref=quad.at[me], dst_ref=quad.at[me], send_sem=sem.at[6], recv_sem=sem.at[7],
                    device_id=(grp, leaf_peer(j)), device_id_type=MESH,
                ).start()
                return 0

            lax.fori_loop(1, N_LEAF, send_s, 0)

        forward = jnp.zeros((16, ROWS_DEV), F32)
        for k in range(NEAR):
            forward = forward + mm_t(jnp.concatenate([partners[k], zero], 0).astype(BF16), tiles[k])
        near = self_part + own_part(forward)
        many = ret_recv.at[t, pl.ds(0, N_LEAF - 1)]
        pltpu.make_async_copy(many, many, sem.at[3]).wait()
        near = near + halves(jnp.sum(ret_recv[t].astype(F32), 0)) + noise * v

        many = grp_q.at[t, pl.ds(0, N_GRP - 1)]
        pltpu.make_async_copy(many, many, sem.at[5]).wait()
        row = iota((8, BLK), 0)
        charges = zero
        sums = jnp.zeros((8, 128), F32)
        for g in range(N_GRP):
            tile = grp_q[t, g]
            charges = jnp.where(row == g, jnp.concatenate([tile[0:1], tile[1:2]], 1), charges)
            sums = sums + tile
        totals = [
            jnp.broadcast_to(jnp.sum(jnp.where(lane[:1] == index, sums[2:3], 0.0), 1, keepdims=True), (8, 128))
            for index in range(len(dots))
        ]
        field = jnp.sum(mm(spread(charges), coup[...]), 0, keepdims=True)
        if last:
            far_share = sum_all(jnp.where(row == 0, charge * field, 0.0))
            many = quad.at[pl.ds(0, N_LEAF - 1)]
            pltpu.make_async_copy(many, many, sem.at[7]).wait()
            grp_s[grp] = jnp.sum(quad[...], 0) + far_share[:1]

            def send_c(j, _):
                pltpu.make_async_remote_copy(
                    src_ref=grp_s.at[grp], dst_ref=grp_s.at[grp], send_sem=sem.at[8], recv_sem=sem.at[9],
                    device_id=(grp_peer(j), me), device_id_type=MESH,
                ).start()
                return 0

            lax.fori_loop(1, N_GRP, send_c, 0)
        far = own_part(mm_t(rows16(jnp.broadcast_to(field, (8, BLK))), tiles[NEAR]))
        quadratic = None
        if last:
            many = grp_s.at[pl.ds(0, N_GRP - 1)]
            pltpu.make_async_copy(many, many, sem.at[9]).wait()
            quadratic = jnp.broadcast_to(jnp.sum(grp_s[...], 0), (8, 128))
        waits = [
            (0, msg_a.at[t, pl.ds(0, N_LEAF - 1)]),
            (2, ret_recv.at[t, pl.ds(0, N_LEAF - 1)]),
            (4, grp_q.at[t, pl.ds(0, N_GRP - 1)]),
        ]
        if last:
            waits += [(6, quad.at[pl.ds(0, N_LEAF - 1)]), (8, grp_s.at[pl.ds(0, N_GRP - 1)])]
        for index, sent in waits:
            pltpu.make_async_copy(sent, sent, sem.at[index]).wait()
        return near + far, totals, quadratic

    def step(t, carry):
        x, r, p, s, z, w, gamma_old, energy_old = carry
        first = t == 0
        u = r * precond
        made, (gamma, delta, mixed), _ = apply(t, jnp.where(first, u, w * precond), (r * u, u * w, u * s), False)
        beta = jnp.where(t <= 1, jnp.zeros_like(gamma), gamma / gamma_old)
        energy = delta + 2.0 * beta * mixed + beta * beta * energy_old
        alpha = wide(jnp.where(first, jnp.zeros_like(gamma), gamma / energy))
        beta = wide(beta)
        p = jnp.where(first, zero, u + beta * p)
        s = jnp.where(first, zero, w + beta * s)
        z = jnp.where(first, zero, made + beta * z)
        w = jnp.where(first, made, w - alpha * z)
        return x + alpha * p, r - alpha * s, p, s, z, w, gamma, energy

    x, r, p, s, z, w, gamma_old, energy_old = lax.fori_loop(
        0, ITERS - 1, step, (zero, right, zero, zero, zero, zero, one, one)
    )
    u, m, q = r * precond, w * precond, s * precond
    made, sums, m_am = apply(
        ITERS - 1, m, (r * u, u * w, u * s, u * z, m * w, m * z, q * w, q * z, q * s), True
    )
    gamma, delta, mixed, uz, mw, mz, qw, qz, qs = sums
    beta = gamma / gamma_old
    energy = delta + 2.0 * beta * mixed + beta * beta * energy_old
    alpha = gamma / energy
    ss = mw + beta * (2.0 * qw + beta * qs)
    ru = delta + beta * mixed
    gamma_last = gamma - alpha * (2.0 * ru - alpha * ss)
    delta_last = delta - alpha * (2.0 * mw + beta * (uz + qw) - alpha * (m_am + beta * (2.0 * mz + beta * qz)))
    beta_last = gamma_last / gamma
    energy_last = delta_last + beta_last * (2.0 * (ru - alpha * ss) + beta_last * energy)
    alpha_last, alpha, beta, beta_last = (wide(a) for a in (gamma_last / energy_last, alpha, beta, beta_last))
    p = u + beta * p
    s = w + beta * s
    z = made + beta * z
    w = w - alpha * z
    x = x + alpha * p
    r = r - alpha * s
    p = r * precond + beta_last * p
    s = w + beta_last * s
    x = x + alpha_last * p
    r = r - alpha_last * s
    for ref, values in ((x_out, x), (r_out, r)):
        ref[pl.ds(0, 8, stride=2), :] = values[:, :128]
        ref[pl.ds(1, 8, stride=2), :] = values[:, 128:]


def on_device(
    configs, order, w_in, bias_in, w_out, noise, right_side, near_blocks, near_live, skeleton
):
    vmem = pl.BlockSpec(memory_space=pltpu.VMEM)
    smem = pl.BlockSpec(memory_space=pltpu.SMEM)
    dma = pltpu.SemaphoreType.DMA
    solution_, residual_ = pl.pallas_call(
        body,
        out_shape=[jax.ShapeDtypeStruct((16, 128), F32)] * 2,
        in_specs=[vmem] * 10 + [smem],
        out_specs=[vmem] * 2,
        scratch_shapes=[
            pltpu.VMEM((N_LEAF * OWN, 64, BLK), BF16),
            pltpu.VMEM((NEAR + 2, ROWS_DEV, BLK), BF16),
            pltpu.VMEM((N_GRP * BLK, BLK), BF16),
            pltpu.VMEM((OWN, BLK, 128), BF16),
            pltpu.VMEM((16, 8, 128), F32),
            pltpu.VMEM((N_LEAF, 8, 128), F32),
            pltpu.VMEM((16, 8, 128), F32),
            pltpu.VMEM((N_GRP, 64, BLK), BF16),
            pltpu.VMEM((128, 512), F32),
            pltpu.VMEM((512, 128), BF16),
            pltpu.VMEM((ITERS, N_LEAF, 32, 128), BF16),
            pltpu.VMEM((ITERS, N_LEAF, 16, 128), BF16),
            pltpu.VMEM((ITERS, N_LEAF, 16, 128), BF16),
            pltpu.VMEM((N_LEAF, 1, 128), F32),
            pltpu.VMEM((ITERS, N_GRP, 8, 128), F32),
            pltpu.VMEM((N_GRP, 1, 128), F32),
            dma((2, 20)),
            dma((2, 20)),
            dma((2, 16)),
            dma((2, 16)),
            dma((6,)),
            dma((ITERS, 10)),
        ],
        compiler_params=pltpu.CompilerParams(
            collective_id=0, has_side_effects=True, vmem_limit_bytes=56 * 2**20
        ),
        cost_estimate=pl.CostEstimate(flops=10**10, bytes_accessed=10**7, transcendentals=10**7),
    )(
        configs.T, order, w_in, bias_in.reshape(1, 128), w_out,
        noise.reshape(16, 128), right_side.reshape(16, 128), near_blocks, near_live, skeleton, near_blocks,
    )
    return solution_.reshape(-1), residual_.reshape(-1)


def solution(mesh):
    in_specs = (
        P(("grp", "leaf"), None),
        P(("grp", "leaf"), None),
        P(),
        P(),
        P(),
        P(("grp", "leaf")),
        P(("grp", "leaf")),
        P(("grp", "leaf"), None),
        P(("grp", "leaf"), None),
        P("grp", None),
    )
    out_specs = (P(("grp", "leaf")), P(("grp", "leaf")))
    return jax.shard_map(
        on_device, mesh=mesh, in_specs=in_specs, out_specs=out_specs, check_vma=False
    )
```

```python
import jax
import jax.numpy as jnp
from jax import lax
from jax.experimental import pallas as pl
from jax.experimental.pallas import tpu as pltpu
from jax.sharding import PartitionSpec as P

BLK = 256
NEAR = 6
ITERS = 4
N_GRP = 8
N_LEAF = 32
OWN = 8
ROWS_DEV = OWN * BLK
F32 = jnp.float32
BF16 = jnp.bfloat16
MESH = pl.DeviceIdType.MESH
SHARP = 10.0 * 1.4426950408889634


def mm(left, right):
    return lax.dot_general(left, right, (((1,), (0,)), ((), ())), preferred_element_type=F32)


def mm_t(left, right):
    return lax.dot_general(left, right, (((1,), (1,)), ((), ())), preferred_element_type=F32)


def iota(shape, dim):
    return lax.broadcasted_iota(jnp.int32, shape, dim)


def kernel_of(inner):
    return jnp.exp2(inner * SHARP - SHARP)


def one_hot(row, base):
    hit = jnp.broadcast_to(row, (BLK, BLK)) == iota((BLK, BLK), 0) + base
    return jnp.where(hit, 1.0, 0.0).astype(BF16)


def flip(values):
    return jnp.transpose(values.astype(F32)).astype(BF16)


def split2(values):
    high = values.astype(BF16).astype(F32)
    return high, (values - high).astype(BF16).astype(F32)


def rows16(values):
    return jnp.concatenate(split2(values), 0).astype(BF16)


def spread(values):
    wide = jnp.concatenate([jnp.concatenate(split2(values), 0)] * OWN, 1)
    shape = (16, ROWS_DEV)
    keep = (iota(shape, 0) & 7) == (iota(shape, 1) >> 8)
    return jnp.where(keep, wide, 0.0).astype(BF16)


def own_part(wide):
    both = wide[:8] + wide[8:]
    row = iota((8, BLK), 0)
    total = jnp.zeros((8, BLK), F32)
    for n in range(OWN):
        total = total + jnp.where(row == n, both[:, n * BLK : (n + 1) * BLK], 0.0)
    return total


def halves(values):
    return jnp.concatenate([values[:8], values[8:]], 1)


def sum_all(values):
    folded = values[:, :128] + values[:, 128:]
    return jnp.broadcast_to(jnp.sum(folded, (0, 1), keepdims=True), (8, 128))


def wide(values):
    return jnp.concatenate([values, values], 1)


def column_of(row):
    return jnp.transpose(jnp.broadcast_to(row.astype(F32), (128, 128)))


def body(
    cfg_ref, order_ref, w_in_ref, bias_ref, w_out_ref, noise_ref, rhs_ref, nb_ref, live_ref, skel_ref,
    nb_s,
    x_out, r_out,
    grp_cfg, tiles, coup, own_feat, part_send, part_recv, skel_tiles, skel_cfg, pick, pick_t,
    msg_a, ret_send, ret_recv, quad, grp_q, grp_s,
    g_send, g_recv, s_send, s_recv, k_sem, it_sem,
):
    grp = lax.axis_index("grp")
    me = lax.axis_index("leaf")
    core = lax.rem(me, 2)
    xx = lax.rem(me // 2, 4)
    yy = me // 8

    def leaf_at(y, x, c):
        return lax.rem(y + 4, 4) * 8 + lax.rem(x + 4, 4) * 2 + c

    def leaf_peer(j):
        return lax.rem(me + j, N_LEAF)

    def grp_peer(j):
        return lax.rem(grp + j, N_GRP)

    barrier = pltpu.get_barrier_semaphore()

    def greet_leaf(j, _):
        pl.semaphore_signal(barrier, inc=1, device_id=(grp, leaf_peer(j)), device_id_type=MESH)
        return 0

    def greet_grp(j, _):
        pl.semaphore_signal(barrier, inc=1, device_id=(grp_peer(j), me), device_id_type=MESH)
        return 0

    lax.fori_loop(1, N_LEAF, greet_leaf, 0)
    lax.fori_loop(1, N_GRP, greet_grp, 0)

    def permute(b, _):
        row = order_ref[:, pl.ds(pl.multiple_of(b * BLK, BLK), BLK)]
        total = jnp.zeros((64, BLK), F32)
        for c in range(OWN):
            total = total + mm(cfg_ref[:, c * BLK : (c + 1) * BLK], one_hot(row, c * BLK))
        grp_cfg[me * OWN + b] = total.astype(BF16)
        return 0

    def at(half, first, second):
        return leaf_at(yy + second, xx + first, core) if half == 0 else leaf_at(yy + first, xx + second, core)

    def piece(leaf, half, quarter=None):
        if quarter is None:
            return grp_cfg.at[pl.ds(leaf * OWN + 4 * half, 4)]
        return grp_cfg.at[pl.ds(leaf * OWN + 4 * half + 2 * quarter, 2)]

    def hop(half, index, ref, target):
        return pltpu.make_async_remote_copy(
            src_ref=ref, dst_ref=ref, send_sem=g_send.at[half, index], recv_sem=g_recv.at[half, index],
            device_id=(grp, target), device_id_type=MESH,
        )

    sibling = me - core + lax.rem(core + 1, 2)

    def to_sibling(half, index, leaf):
        ref = piece(leaf, half)
        copy = pltpu.make_async_remote_copy(
            src_ref=ref, dst_ref=ref, send_sem=s_send.at[half, index], recv_sem=s_recv.at[half, index],
            device_id=(grp, sibling), device_id_type=MESH,
        )
        copy.start()
        return copy

    started = []

    def start(copy):
        copy.start()
        started.append(copy)

    offsets = (0, -1, 1, 2)

    def second_axis(half, p):
        ref = piece(at(half, offsets[p], 0), half)
        start(hop(half, 4 + 4 * p, ref, at(half, 0, 1)))
        start(hop(half, 5 + 4 * p, ref, at(half, 0, -1)))
        started.append(to_sibling(half, 4 * p, at(half, offsets[p], 0)))

    def arrived(half, index, ref):
        hop(half, index, ref, me).wait_recv()

    for half in range(2):
        lax.fori_loop(4 * half, 4 * half + 4, permute, 0)
        if half == 0:
            pl.semaphore_wait(barrier, N_LEAF - 1 + N_GRP - 1)
        own = piece(me, half)
        start(hop(half, 0, own, at(half, 1, 0)))
        start(hop(half, 1, own, at(half, -1, 0)))

    def choose(b, total):
        return total + mm(grp_cfg[me * OWN + b], one_hot(skel_ref[...] - me * ROWS_DEV, b * BLK))

    given = lax.fori_loop(0, OWN, choose, jnp.zeros((64, BLK), F32))
    for q in range(16):
        part_send[q] = given[q // 2 * 8 : q // 2 * 8 + 8, q % 2 * 128 : q % 2 * 128 + 128]
    part_recv[me] = part_send[me // 2]

    def send_part(j, _):
        peer = leaf_peer(j)
        pltpu.make_async_remote_copy(
            src_ref=part_send.at[peer // 2], dst_ref=part_recv.at[me], send_sem=k_sem.at[0], recv_sem=k_sem.at[1],
            device_id=(grp, peer), device_id_type=MESH,
        ).start()
        return 0

    lax.fori_loop(1, N_LEAF, send_part, 0)
    for half in range(2):
        second_axis(half, 0)

    w_in_t = flip(w_in_ref[...])
    w_out_t = flip(w_out_ref[...])
    bias = column_of(bias_ref[...])

    def features(configs):
        hidden = mm(w_in_t, configs)
        hidden = jnp.tanh(hidden + jnp.concatenate([bias] * (configs.shape[1] // 128), 1)).astype(BF16)
        raw = mm(w_out_t, hidden)
        return (raw * lax.rsqrt(jnp.sum(raw * raw, 0, keepdims=True) + 1e-06)).astype(BF16)

    def own_row(n, _):
        feat_t = features(grp_cfg[me * OWN + n])
        feat = flip(feat_t)
        own_feat[n] = feat
        tiles[NEAR + 1, pl.ds(n * BLK, BLK), :] = kernel_of(mm(feat, feat_t)).astype(BF16)
        return 0

    def sum_parts():
        many = part_recv.at[pl.ds(0, N_LEAF - 1)]
        pltpu.make_async_copy(many, many, k_sem.at[1]).wait()
        skel_tiles[me // 2] = jnp.sum(part_recv[...], 0)

        def send_tile(j, _):
            pltpu.make_async_remote_copy(
                src_ref=skel_tiles.at[me // 2], dst_ref=skel_tiles.at[me // 2], send_sem=k_sem.at[2], recv_sem=k_sem.at[3],
                device_id=(grp, leaf_peer(2 * j)), device_id_type=MESH,
            ).start()
            return 0

        lax.fori_loop(1, N_LEAF // 2, send_tile, 0)

    def send_skeleton():
        many = skel_tiles.at[pl.ds(0, N_LEAF // 2 - 1)]
        pltpu.make_async_copy(many, many, k_sem.at[3]).wait()
        for h in range(2):
            skel_cfg[grp, :, h * 128 : (h + 1) * 128] = jnp.concatenate(
                [skel_tiles[2 * q + h] for q in range(8)], 0
            ).astype(BF16)

        def send_skel(j, _):
            pltpu.make_async_remote_copy(
                src_ref=skel_cfg.at[grp], dst_ref=skel_cfg.at[grp], send_sem=k_sem.at[4], recv_sem=k_sem.at[5],
                device_id=(grp_peer(j), me), device_id_type=MESH,
            ).start()
            return 0

        lax.fori_loop(1, N_GRP, send_skel, 0)

    def make_basis():
        skel_t = features(skel_cfg[grp])

        def basis(n, _):
            tiles[NEAR, pl.ds(n * BLK, BLK), :] = kernel_of(mm(own_feat[n], skel_t)).astype(BF16)
            return 0

        lax.fori_loop(0, OWN, basis, 0)
        return skel_t

    def make_couplings(skel_t):
        many = skel_cfg.at[pl.ds(0, N_GRP - 1)]
        pltpu.make_async_copy(many, many, k_sem.at[5]).wait()

        def couple(g, _):
            coup[pl.ds(g * BLK, BLK), :] = kernel_of(mm(flip(features(skel_cfg[g])), skel_t)).astype(BF16)
            return 0

        lax.fori_loop(0, N_GRP, couple, 0)

    nb = nb_ref[...]
    live = live_ref[...].astype(F32)
    place = nb + (nb & -8)
    for h in range(2):
        for k in range(NEAR):
            hit = iota((8, 512), 1) == place[:, k : k + 1] + 8 * h
            pick[pl.ds((h * NEAR + k) * 8, 8), :] = jnp.where(hit, live[:, k : k + 1], 0.0)
    pick[pl.ds(96, 32), :] = jnp.zeros((32, 512), F32)
    for q in range(4):
        pick_t[pl.ds(q * 128, 128), :] = jnp.transpose(pick[:, q * 128 : (q + 1) * 128]).astype(BF16)
    count = jnp.zeros((8, BLK), F32)
    for k in range(NEAR):
        count = count + jnp.where(iota((8, BLK), 1) == nb[:, k : k + 1], live[:, k : k + 1], 0.0)
    count = jnp.sum(count, 0, keepdims=True)
    own_uses = jnp.sum(live, 1, keepdims=True)

    noise = jnp.concatenate([noise_ref[pl.ds(0, 8, stride=2), :], noise_ref[pl.ds(1, 8, stride=2), :]], 1)
    target = jnp.concatenate([rhs_ref[pl.ds(0, 8, stride=2), :], rhs_ref[pl.ds(1, 8, stride=2), :]], 1)
    precond = 1.0 / (1.0 + noise)
    zero = jnp.zeros((8, BLK), F32)
    one = jnp.ones((8, 128), F32)

    def send_vector(t, v, dots):
        sem = it_sem.at[t]
        v_wide = spread(v)
        charge = jnp.sum(mm(v_wide, tiles[NEAR]), 0, keepdims=True)

        c_high, c_mid = split2(charge)
        rows = [c_high[:, :128], c_high[:, 128:], c_mid[:, :128], c_mid[:, 128:], count[:, :128], count[:, 128:]]
        lane = iota((8, 128), 1)
        sums = jnp.zeros((8, 128), F32)
        for index, values in enumerate(dots):
            sums = jnp.where(lane == index, sum_all(values), sums)
        s_high, s_mid = split2(sums)
        rows += [s_high[:1], s_mid[:1], (sums - s_high - s_mid)[:1]]
        row = iota((16, 128), 0)
        extra = jnp.zeros((16, 128), F32)
        for at_row, values in enumerate(rows):
            extra = jnp.where(row == at_row, values, extra)
        msg_a[t, me, pl.ds(0, 16), :] = jnp.concatenate([v[:, :128], v[:, 128:]], 0).astype(BF16)
        msg_a[t, me, pl.ds(16, 16), :] = extra.astype(BF16)

        def send_a(j, _):
            pltpu.make_async_remote_copy(
                src_ref=msg_a.at[t, me], dst_ref=msg_a.at[t, me], send_sem=sem.at[0], recv_sem=sem.at[1],
                device_id=(grp, leaf_peer(j)), device_id_type=MESH,
            ).start()
            return 0

        lax.fori_loop(1, N_LEAF, send_a, 0)
        return v_wide

    def send_returns(t, v_wide):
        sem = it_sem.at[t]
        backs = []
        for k in range(NEAR):
            made = mm(v_wide, tiles[k])
            backs.append(made[:8] + made[8:])
        stack = jnp.concatenate([b[:, :128] for b in backs] + [b[:, 128:] for b in backs] + [jnp.zeros((32, 128), F32)], 0)
        b_high, b_mid = split2(stack)
        returned = mm(pick_t[...], b_high.astype(BF16)) + mm(pick_t[...], b_mid.astype(BF16))
        ret_send[t] = returned.reshape(N_LEAF, 16, 128).astype(BF16)
        ret_recv[t, me] = ret_send[t, me]

        def send_r(j, _):
            peer = leaf_peer(j)
            pltpu.make_async_remote_copy(
                src_ref=ret_send.at[t, peer], dst_ref=ret_recv.at[t, me], send_sem=sem.at[2], recv_sem=sem.at[3],
                device_id=(grp, peer), device_id_type=MESH,
            ).start()
            return 0

        lax.fori_loop(1, N_LEAF, send_r, 0)
        made = mm(v_wide, tiles[NEAR + 1])
        return backs, made[:8] + made[8:]

    def pass_charges(t):
        sem = it_sem.at[t]
        many = msg_a.at[t, pl.ds(0, N_LEAF - 1)]
        pltpu.make_async_copy(many, many, sem.at[1]).wait()
        extra = jnp.sum(msg_a[t, :, pl.ds(16, 16), :].astype(F32), 0)
        charge = jnp.concatenate([extra[0:1] + extra[2:3], extra[1:2] + extra[3:4]], 1)
        row = iota((8, 128), 0)
        tile = jnp.where(row == 0, charge[:, :128], 0.0)
        tile = jnp.where(row == 1, charge[:, 128:], tile)
        tile = jnp.where(row == 2, extra[6:7] + extra[7:8] + extra[8:9], tile)
        grp_q[t, grp] = tile

        def send_q(j, _):
            pltpu.make_async_remote_copy(
                src_ref=grp_q.at[t, grp], dst_ref=grp_q.at[t, grp], send_sem=sem.at[4], recv_sem=sem.at[5],
                device_id=(grp_peer(j), me), device_id_type=MESH,
            ).start()
            return 0

        lax.fori_loop(1, N_GRP, send_q, 0)
        return charge, extra

    def finish(t, v, terms, group, n_dots, last):
        sem = it_sem.at[t]
        backs, self_part = terms
        charge, extra = group
        lane = iota((8, 128), 1)
        counts = jnp.broadcast_to(jnp.concatenate([extra[4:5], extra[5:6]], 1), (8, BLK))
        mine = iota((8, BLK), 1) == me * OWN + iota((8, BLK), 0)
        weight = own_uses + jnp.sum(jnp.where(mine, counts, 0.0), 1, keepdims=True)
        self_part = weight * self_part
        vectors = msg_a[t, :, pl.ds(0, 16), :].reshape(N_LEAF * 16, 128)
        found = mm(pick[...].astype(BF16), vectors)
        partners = [
            jnp.concatenate([found[k * 8 : k * 8 + 8], found[(NEAR + k) * 8 : (NEAR + k) * 8 + 8]], 1) for k in range(NEAR)
        ]
        if last:
            share = v * (self_part + noise * v)
            for k in range(NEAR):
                share = share + 2.0 * backs[k] * partners[k]
            quad[me] = sum_all(share)[:1]

            def send_s(j, _):
                pltpu.make_async_remote_copy(
                    src_ref=quad.at[me], dst_ref=quad.at[me], send_sem=sem.at[6], recv_sem=sem.at[7],
                    device_id=(grp, leaf_peer(j)), device_id_type=MESH,
                ).start()
                return 0

            lax.fori_loop(1, N_LEAF, send_s, 0)

        forward = jnp.zeros((16, ROWS_DEV), F32)
        for k in range(NEAR):
            forward = forward + mm_t(jnp.concatenate([partners[k], zero], 0).astype(BF16), tiles[k])
        near = self_part + own_part(forward)
        many = ret_recv.at[t, pl.ds(0, N_LEAF - 1)]
        pltpu.make_async_copy(many, many, sem.at[3]).wait()
        near = near + halves(jnp.sum(ret_recv[t].astype(F32), 0)) + noise * v

        many = grp_q.at[t, pl.ds(0, N_GRP - 1)]
        pltpu.make_async_copy(many, many, sem.at[5]).wait()
        row = iota((8, BLK), 0)
        charges = zero
        sums = jnp.zeros((8, 128), F32)
        for g in range(N_GRP):
            tile = grp_q[t, g]
            charges = jnp.where(row == g, jnp.concatenate([tile[0:1], tile[1:2]], 1), charges)
            sums = sums + tile
        totals = [
            jnp.broadcast_to(jnp.sum(jnp.where(lane[:1] == index, sums[2:3], 0.0), 1, keepdims=True), (8, 128))
            for index in range(n_dots)
        ]
        field = jnp.sum(mm(spread(charges), coup[...]), 0, keepdims=True)
        if last:
            far_share = sum_all(jnp.where(row == 0, charge * field, 0.0))
            many = quad.at[pl.ds(0, N_LEAF - 1)]
            pltpu.make_async_copy(many, many, sem.at[7]).wait()
            grp_s[grp] = jnp.sum(quad[...], 0) + far_share[:1]

            def send_c(j, _):
                pltpu.make_async_remote_copy(
                    src_ref=grp_s.at[grp], dst_ref=grp_s.at[grp], send_sem=sem.at[8], recv_sem=sem.at[9],
                    device_id=(grp_peer(j), me), device_id_type=MESH,
                ).start()
                return 0

            lax.fori_loop(1, N_GRP, send_c, 0)
        far = own_part(mm_t(rows16(jnp.broadcast_to(field, (8, BLK))), tiles[NEAR]))
        quadratic = None
        if last:
            many = grp_s.at[pl.ds(0, N_GRP - 1)]
            pltpu.make_async_copy(many, many, sem.at[9]).wait()
            quadratic = jnp.broadcast_to(jnp.sum(grp_s[...], 0), (8, 128))
        waits = [
            (0, msg_a.at[t, pl.ds(0, N_LEAF - 1)]),
            (2, ret_recv.at[t, pl.ds(0, N_LEAF - 1)]),
            (4, grp_q.at[t, pl.ds(0, N_GRP - 1)]),
        ]
        if last:
            waits += [(6, quad.at[pl.ds(0, N_LEAF - 1)]), (8, grp_s.at[pl.ds(0, N_GRP - 1)])]
        for index, sent in waits:
            pltpu.make_async_copy(sent, sent, sem.at[index]).wait()
        return near + far, totals, quadratic

    def apply(t, v, dots, last):
        v_wide = send_vector(t, v, dots)
        terms = send_returns(t, v_wide)
        return finish(t, v, terms, pass_charges(t), len(dots), last)

    lax.fori_loop(0, OWN, own_row, 0)
    for half in range(2):
        left, right = at(half, -1, 0), at(half, 1, 0)
        arrived(half, 0, piece(left, half))
        start(hop(half, 2, piece(left, half, 0), right))
        arrived(half, 1, piece(right, half))
        start(hop(half, 3, piece(right, half, 1), left))
    for half in range(2):
        second_axis(half, 1)
        second_axis(half, 2)
    sum_parts()
    for p in range(4):
        if p == 1:
            for half in range(2):
                far = at(half, 2, 0)
                arrived(half, 2, piece(far, half, 0))
                arrived(half, 3, piece(far, half, 1))
                second_axis(half, 3)
            send_skeleton()
        for half in range(2):
            down, up = at(half, offsets[p], -1), at(half, offsets[p], 1)
            arrived(half, 4 + 4 * p, piece(down, half))
            start(hop(half, 6 + 4 * p, piece(down, half, 0), at(half, 0, 1)))
            started.append(to_sibling(half, 4 * p + 1, down))
            arrived(half, 5 + 4 * p, piece(up, half))
            start(hop(half, 7 + 4 * p, piece(up, half, 1), at(half, 0, -1)))
            started.append(to_sibling(half, 4 * p + 2, up))
        if p == 2:
            skel_t = make_basis()
    for p in range(4):
        if p == 3:
            make_couplings(skel_t)
        for half in range(2):
            over = at(half, offsets[p], 2)
            arrived(half, 6 + 4 * p, piece(over, half, 0))
            arrived(half, 7 + 4 * p, piece(over, half, 1))
            started.append(to_sibling(half, 4 * p + 3, over))
    first = target * precond
    first_wide = send_vector(0, first, ())
    steps = (0, -1, 1, 2)
    for p in range(4):
        for half in range(2):
            for s in range(4):
                theirs = at(half, offsets[p], steps[s]) - core + lax.rem(core + 1, 2)
                ref = piece(theirs, half)
                pltpu.make_async_remote_copy(
                    src_ref=ref, dst_ref=ref, send_sem=s_send.at[half, 4 * p + s], recv_sem=s_recv.at[half, 4 * p + s],
                    device_id=(grp, sibling), device_id_type=MESH,
                ).wait_recv()
    for copy in started:
        copy.wait_send()

    def tile_row(n, _):
        feat_t = features(jnp.concatenate([grp_cfg[nb_s[n, k]] for k in range(NEAR)], 1))
        made = kernel_of(mm(own_feat[n], feat_t)).astype(BF16)
        for k in range(NEAR):
            tiles[k, pl.ds(n * BLK, BLK), :] = made[:, k * BLK : (k + 1) * BLK]
        return 0

    lax.fori_loop(0, OWN, tile_row, 0)
    first_group = pass_charges(0)

    for index, sent in (
        (0, part_recv.at[pl.ds(0, N_LEAF - 1)]),
        (2, skel_tiles.at[pl.ds(0, N_LEAF // 2 - 1)]),
        (4, skel_cfg.at[pl.ds(0, N_GRP - 1)]),
    ):
        pltpu.make_async_copy(sent, sent, k_sem.at[index]).wait()

    w, _, _ = finish(0, first, send_returns(0, first_wide), first_group, 0, False)

    def step(t, carry):
        x, r, p, s, z, w, gamma_old, energy_old = carry
        u = r * precond
        made, (gamma, delta, mixed), _ = apply(t, w * precond, (r * u, u * w, u * s), False)
        beta = jnp.where(t == 1, jnp.zeros_like(gamma), gamma / gamma_old)
        energy = delta + 2.0 * beta * mixed + beta * beta * energy_old
        alpha = wide(gamma / energy)
        beta = wide(beta)
        p = u + beta * p
        s = w + beta * s
        z = made + beta * z
        return x + alpha * p, r - alpha * s, p, s, z, w - alpha * z, gamma, energy

    x, r, p, s, z, w, gamma_old, energy_old = lax.fori_loop(
        1, ITERS - 1, step, (zero, target, zero, zero, zero, w, one, one)
    )
    u, m, q = r * precond, w * precond, s * precond
    made, sums, m_am = apply(
        ITERS - 1, m, (r * u, u * w, u * s, u * z, m * w, m * z, q * w, q * z, q * s), True
    )
    gamma, delta, mixed, uz, mw, mz, qw, qz, qs = sums
    beta = gamma / gamma_old
    energy = delta + 2.0 * beta * mixed + beta * beta * energy_old
    alpha = gamma / energy
    ss = mw + beta * (2.0 * qw + beta * qs)
    ru = delta + beta * mixed
    gamma_last = gamma - alpha * (2.0 * ru - alpha * ss)
    delta_last = delta - alpha * (2.0 * mw + beta * (uz + qw) - alpha * (m_am + beta * (2.0 * mz + beta * qz)))
    beta_last = gamma_last / gamma
    energy_last = delta_last + beta_last * (2.0 * (ru - alpha * ss) + beta_last * energy)
    alpha_last, alpha, beta, beta_last = (wide(a) for a in (gamma_last / energy_last, alpha, beta, beta_last))
    p = u + beta * p
    s = w + beta * s
    z = made + beta * z
    w = w - alpha * z
    x = x + alpha * p
    r = r - alpha * s
    p = r * precond + beta_last * p
    s = w + beta_last * s
    x = x + alpha_last * p
    r = r - alpha_last * s
    for ref, values in ((x_out, x), (r_out, r)):
        ref[pl.ds(0, 8, stride=2), :] = values[:, :128]
        ref[pl.ds(1, 8, stride=2), :] = values[:, 128:]


def on_device(
    configs, order, w_in, bias_in, w_out, noise, right_side, near_blocks, near_live, skeleton
):
    vmem = pl.BlockSpec(memory_space=pltpu.VMEM)
    smem = pl.BlockSpec(memory_space=pltpu.SMEM)
    dma = pltpu.SemaphoreType.DMA
    solution_, residual_ = pl.pallas_call(
        body,
        out_shape=[jax.ShapeDtypeStruct((16, 128), F32)] * 2,
        in_specs=[vmem] * 10 + [smem],
        out_specs=[vmem] * 2,
        scratch_shapes=[
            pltpu.VMEM((N_LEAF * OWN, 64, BLK), BF16),
            pltpu.VMEM((NEAR + 2, ROWS_DEV, BLK), BF16),
            pltpu.VMEM((N_GRP * BLK, BLK), BF16),
            pltpu.VMEM((OWN, BLK, 128), BF16),
            pltpu.VMEM((16, 8, 128), F32),
            pltpu.VMEM((N_LEAF, 8, 128), F32),
            pltpu.VMEM((16, 8, 128), F32),
            pltpu.VMEM((N_GRP, 64, BLK), BF16),
            pltpu.VMEM((128, 512), F32),
            pltpu.VMEM((512, 128), BF16),
            pltpu.VMEM((ITERS, N_LEAF, 32, 128), BF16),
            pltpu.VMEM((ITERS, N_LEAF, 16, 128), BF16),
            pltpu.VMEM((ITERS, N_LEAF, 16, 128), BF16),
            pltpu.VMEM((N_LEAF, 1, 128), F32),
            pltpu.VMEM((ITERS, N_GRP, 8, 128), F32),
            pltpu.VMEM((N_GRP, 1, 128), F32),
            dma((2, 20)),
            dma((2, 20)),
            dma((2, 16)),
            dma((2, 16)),
            dma((6,)),
            dma((ITERS, 10)),
        ],
        compiler_params=pltpu.CompilerParams(
            collective_id=0, has_side_effects=True, vmem_limit_bytes=56 * 2**20
        ),
        cost_estimate=pl.CostEstimate(flops=10**10, bytes_accessed=10**7, transcendentals=10**7),
    )(
        configs.T, order, w_in, bias_in.reshape(1, 128), w_out,
        noise.reshape(16, 128), right_side.reshape(16, 128), near_blocks, near_live, skeleton, near_blocks,
    )
    return solution_.reshape(-1), residual_.reshape(-1)


def solution(mesh):
    in_specs = (
        P(("grp", "leaf"), None),
        P(("grp", "leaf"), None),
        P(),
        P(),
        P(),
        P(("grp", "leaf")),
        P(("grp", "leaf")),
        P(("grp", "leaf"), None),
        P(("grp", "leaf"), None),
        P("grp", None),
    )
    out_specs = (P(("grp", "leaf")), P(("grp", "leaf")))
    return jax.shard_map(
        on_device, mesh=mesh, in_specs=in_specs, out_specs=out_specs, check_vma=False
    )
```

```python
import jax
import jax.numpy as jnp
from jax import lax
from jax.experimental import pallas as pl
from jax.experimental.pallas import tpu as pltpu
from jax.sharding import PartitionSpec as P

BLK = 256
NEAR = 6
ITERS = 4
N_GRP = 8
N_LEAF = 32
OWN = 8
ROWS_DEV = OWN * BLK
F32 = jnp.float32
BF16 = jnp.bfloat16
MESH = pl.DeviceIdType.MESH
SHARP = 10.0 * 1.4426950408889634


def mm(left, right):
    return lax.dot_general(left, right, (((1,), (0,)), ((), ())), preferred_element_type=F32)


def mm_t(left, right):
    return lax.dot_general(left, right, (((1,), (1,)), ((), ())), preferred_element_type=F32)


def iota(shape, dim):
    return lax.broadcasted_iota(jnp.int32, shape, dim)


def kernel_of(inner):
    return jnp.exp2(inner * SHARP - SHARP)


def one_hot(row, base):
    hit = jnp.broadcast_to(row, (BLK, BLK)) == iota((BLK, BLK), 0) + base
    return jnp.where(hit, 1.0, 0.0).astype(BF16)


def flip(values):
    return jnp.transpose(values.astype(F32)).astype(BF16)


def split2(values):
    high = values.astype(BF16).astype(F32)
    return high, (values - high).astype(BF16).astype(F32)


def rows16(values):
    return jnp.concatenate(split2(values), 0).astype(BF16)


def spread(values):
    wide = jnp.concatenate([jnp.concatenate(split2(values), 0)] * OWN, 1)
    shape = (16, ROWS_DEV)
    keep = (iota(shape, 0) & 7) == (iota(shape, 1) >> 8)
    return jnp.where(keep, wide, 0.0).astype(BF16)


def own_part(wide):
    both = wide[:8] + wide[8:]
    row = iota((8, BLK), 0)
    total = jnp.zeros((8, BLK), F32)
    for n in range(OWN):
        total = total + jnp.where(row == n, both[:, n * BLK : (n + 1) * BLK], 0.0)
    return total


def halves(values):
    return jnp.concatenate([values[:8], values[8:]], 1)


def sum_all(values):
    folded = values[:, :128] + values[:, 128:]
    return jnp.broadcast_to(jnp.sum(folded, (0, 1), keepdims=True), (8, 128))


def wide(values):
    return jnp.concatenate([values, values], 1)


def column_of(row):
    return jnp.transpose(jnp.broadcast_to(row.astype(F32), (128, 128)))


def body(
    cfg_ref, order_ref, w_in_ref, bias_ref, w_out_ref, noise_ref, rhs_ref, nb_ref, live_ref, skel_ref,
    nb_s,
    xr_out,
    grp_cfg, tiles, coup, own_feat, part_send, part_recv, skel_tiles, skel_cfg, pick, pick_t,
    msg_q, msg_v, ret_send, ret_recv, quad, grp_q, grp_s,
    g_send, g_recv, s_send, s_recv, k_sem, it_sem,
):
    grp = lax.axis_index("grp")
    me = lax.axis_index("leaf")
    core = lax.rem(me, 2)
    xx = lax.rem(me // 2, 4)
    yy = me // 8

    def leaf_at(y, x, c):
        return lax.rem(y + 4, 4) * 8 + lax.rem(x + 4, 4) * 2 + c

    def leaf_peer(j):
        return lax.rem(me + j, N_LEAF)

    def grp_peer(j):
        return lax.rem(grp + j, N_GRP)

    barrier = pltpu.get_barrier_semaphore()

    def greet_leaf(j, _):
        pl.semaphore_signal(barrier, inc=1, device_id=(grp, leaf_peer(j)), device_id_type=MESH)
        return 0

    def greet_grp(j, _):
        pl.semaphore_signal(barrier, inc=1, device_id=(grp_peer(j), me), device_id_type=MESH)
        return 0

    lax.fori_loop(1, N_LEAF, greet_leaf, 0)
    lax.fori_loop(1, N_GRP, greet_grp, 0)

    def permute(b, _):
        row = order_ref[:, pl.ds(pl.multiple_of(b * BLK, BLK), BLK)]
        total = jnp.zeros((64, BLK), F32)
        for c in range(OWN):
            total = total + mm(cfg_ref[:, c * BLK : (c + 1) * BLK], one_hot(row, c * BLK))
        grp_cfg[me * OWN + b] = total.astype(BF16)
        return 0

    def at(half, first, second):
        return leaf_at(yy + second, xx + first, core) if half == 0 else leaf_at(yy + first, xx + second, core)

    def piece(leaf, half, quarter=None):
        if quarter is None:
            return grp_cfg.at[pl.ds(leaf * OWN + 4 * half, 4)]
        return grp_cfg.at[pl.ds(leaf * OWN + 4 * half + 2 * quarter, 2)]

    def hop(half, index, ref, target):
        return pltpu.make_async_remote_copy(
            src_ref=ref, dst_ref=ref, send_sem=g_send.at[half, index], recv_sem=g_recv.at[half, index],
            device_id=(grp, target), device_id_type=MESH,
        )

    sibling = me - core + lax.rem(core + 1, 2)

    def to_sibling(half, index, leaf):
        ref = piece(leaf, half)
        copy = pltpu.make_async_remote_copy(
            src_ref=ref, dst_ref=ref, send_sem=s_send.at[half, index], recv_sem=s_recv.at[half, index],
            device_id=(grp, sibling), device_id_type=MESH,
        )
        copy.start()
        return copy

    started = []

    def start(copy):
        copy.start()
        started.append(copy)

    offsets = (0, -1, 1, 2)

    def second_axis(half, p):
        ref = piece(at(half, offsets[p], 0), half)
        start(hop(half, 4 + 4 * p, ref, at(half, 0, 1)))
        start(hop(half, 5 + 4 * p, ref, at(half, 0, -1)))
        started.append(to_sibling(half, 4 * p, at(half, offsets[p], 0)))

    def arrived(half, index, ref):
        hop(half, index, ref, me).wait_recv()

    for half in range(2):
        lax.fori_loop(4 * half, 4 * half + 4, permute, 0)
        if half == 0:
            pl.semaphore_wait(barrier, N_LEAF - 1 + N_GRP - 1)
        own = piece(me, half)
        start(hop(half, 0, own, at(half, 1, 0)))
        start(hop(half, 1, own, at(half, -1, 0)))

    def choose(b, total):
        return total + mm(grp_cfg[me * OWN + b], one_hot(skel_ref[...] - me * ROWS_DEV, b * BLK))

    given = lax.fori_loop(0, OWN, choose, jnp.zeros((64, BLK), F32))
    for q in range(16):
        part_send[q] = given[q // 2 * 8 : q // 2 * 8 + 8, q % 2 * 128 : q % 2 * 128 + 128]
    part_recv[me] = part_send[me // 2]

    def send_part(j, _):
        peer = leaf_peer(j)
        pltpu.make_async_remote_copy(
            src_ref=part_send.at[peer // 2], dst_ref=part_recv.at[me], send_sem=k_sem.at[0], recv_sem=k_sem.at[1],
            device_id=(grp, peer), device_id_type=MESH,
        ).start()
        return 0

    lax.fori_loop(1, N_LEAF, send_part, 0)
    for half in range(2):
        second_axis(half, 0)

    w_in_t = flip(w_in_ref[...])
    w_out_t = flip(w_out_ref[...])
    bias = column_of(bias_ref[...])

    def features(configs):
        hidden = mm(w_in_t, configs)
        hidden = jnp.tanh(hidden + jnp.concatenate([bias] * (configs.shape[1] // 128), 1)).astype(BF16)
        raw = mm(w_out_t, hidden)
        return (raw * lax.rsqrt(jnp.sum(raw * raw, 0, keepdims=True) + 1e-06)).astype(BF16)

    def own_row(n, _):
        feat_t = features(grp_cfg[me * OWN + n])
        feat = flip(feat_t)
        own_feat[n] = feat
        tiles[NEAR + 1, pl.ds(n * BLK, BLK), :] = kernel_of(mm(feat, feat_t)).astype(BF16)
        return 0

    def sum_parts():
        many = part_recv.at[pl.ds(0, N_LEAF - 1)]
        pltpu.make_async_copy(many, many, k_sem.at[1]).wait()
        skel_tiles[me // 2] = jnp.sum(part_recv[...], 0)

        def send_tile(j, _):
            pltpu.make_async_remote_copy(
                src_ref=skel_tiles.at[me // 2], dst_ref=skel_tiles.at[me // 2], send_sem=k_sem.at[2], recv_sem=k_sem.at[3],
                device_id=(grp, leaf_peer(2 * j)), device_id_type=MESH,
            ).start()
            return 0

        lax.fori_loop(1, N_LEAF // 2, send_tile, 0)

    def send_skeleton():
        many = skel_tiles.at[pl.ds(0, N_LEAF // 2 - 1)]
        pltpu.make_async_copy(many, many, k_sem.at[3]).wait()
        for h in range(2):
            skel_cfg[grp, :, h * 128 : (h + 1) * 128] = jnp.concatenate(
                [skel_tiles[2 * q + h] for q in range(8)], 0
            ).astype(BF16)

        def send_skel(j, _):
            pltpu.make_async_remote_copy(
                src_ref=skel_cfg.at[grp], dst_ref=skel_cfg.at[grp], send_sem=k_sem.at[4], recv_sem=k_sem.at[5],
                device_id=(grp_peer(j), me), device_id_type=MESH,
            ).start()
            return 0

        lax.fori_loop(1, N_GRP, send_skel, 0)

    def make_basis():
        skel_t = features(skel_cfg[grp])

        def basis(n, _):
            tiles[NEAR, pl.ds(n * BLK, BLK), :] = kernel_of(mm(own_feat[n], skel_t)).astype(BF16)
            return 0

        lax.fori_loop(0, OWN, basis, 0)
        return skel_t

    def make_couplings(skel_t):
        many = skel_cfg.at[pl.ds(0, N_GRP - 1)]
        pltpu.make_async_copy(many, many, k_sem.at[5]).wait()

        def couple(g, _):
            coup[pl.ds(g * BLK, BLK), :] = kernel_of(mm(flip(features(skel_cfg[g])), skel_t)).astype(BF16)
            return 0

        lax.fori_loop(0, N_GRP, couple, 0)

    nb = nb_ref[...]
    live = live_ref[...].astype(F32)
    place = nb + (nb & -8)
    for h in range(2):
        for k in range(NEAR):
            hit = iota((8, 512), 1) == place[:, k : k + 1] + 8 * h
            pick[pl.ds((h * NEAR + k) * 8, 8), :] = jnp.where(hit, live[:, k : k + 1], 0.0)
    pick[pl.ds(96, 32), :] = jnp.zeros((32, 512), F32)
    for q in range(4):
        pick_t[pl.ds(q * 128, 128), :] = jnp.transpose(pick[:, q * 128 : (q + 1) * 128]).astype(BF16)
    count = jnp.zeros((8, BLK), F32)
    for k in range(NEAR):
        count = count + jnp.where(iota((8, BLK), 1) == nb[:, k : k + 1], live[:, k : k + 1], 0.0)
    count = jnp.sum(count, 0, keepdims=True)
    own_uses = jnp.sum(live, 1, keepdims=True)

    noise = jnp.concatenate([noise_ref[pl.ds(0, 8, stride=2), :], noise_ref[pl.ds(1, 8, stride=2), :]], 1)
    target = jnp.concatenate([rhs_ref[pl.ds(0, 8, stride=2), :], rhs_ref[pl.ds(1, 8, stride=2), :]], 1)
    precond = 1.0 / (1.0 + noise)
    zero = jnp.zeros((8, BLK), F32)
    one = jnp.ones((8, 128), F32)

    def send_vector(t, v, dots):
        sem = it_sem.at[t]
        v_wide = spread(v)
        charge = jnp.sum(mm(v_wide, tiles[NEAR]), 0, keepdims=True)

        c_high, c_mid = split2(charge)
        rows = [c_high[:, :128], c_high[:, 128:], c_mid[:, :128], c_mid[:, 128:], count[:, :128], count[:, 128:]]
        lane = iota((8, 128), 1)
        sums = jnp.zeros((8, 128), F32)
        for index, values in enumerate(dots):
            sums = jnp.where(lane == index, sum_all(values), sums)
        s_high, s_mid = split2(sums)
        rows += [s_high[:1], s_mid[:1], (sums - s_high - s_mid)[:1]]
        row = iota((16, 128), 0)
        extra = jnp.zeros((16, 128), F32)
        for at_row, values in enumerate(rows):
            extra = jnp.where(row == at_row, values, extra)
        msg_q[t, me] = extra.astype(BF16)
        msg_v[t, me] = jnp.concatenate([v[:, :128], v[:, 128:]], 0).astype(BF16)
        for ref, index in ((msg_q, 0), (msg_v, 10)):

            def send_a(j, _, ref=ref, index=index):
                pltpu.make_async_remote_copy(
                    src_ref=ref.at[t, me], dst_ref=ref.at[t, me], send_sem=sem.at[index], recv_sem=sem.at[index + 1],
                    device_id=(grp, leaf_peer(j)), device_id_type=MESH,
                ).start()
                return 0

            lax.fori_loop(1, N_LEAF, send_a, 0)
        return v_wide

    def send_returns(t, v_wide):
        sem = it_sem.at[t]
        backs = []
        for k in range(NEAR):
            made = mm(v_wide, tiles[k])
            backs.append(made[:8] + made[8:])
        stack = jnp.concatenate([b[:, :128] for b in backs] + [b[:, 128:] for b in backs] + [jnp.zeros((32, 128), F32)], 0)
        b_high, b_mid = split2(stack)
        returned = mm(pick_t[...], b_high.astype(BF16)) + mm(pick_t[...], b_mid.astype(BF16))
        ret_send[t] = returned.reshape(N_LEAF, 16, 128).astype(BF16)
        ret_recv[t, me] = ret_send[t, me]

        def send_r(j, _):
            peer = leaf_peer(j)
            pltpu.make_async_remote_copy(
                src_ref=ret_send.at[t, peer], dst_ref=ret_recv.at[t, me], send_sem=sem.at[2], recv_sem=sem.at[3],
                device_id=(grp, peer), device_id_type=MESH,
            ).start()
            return 0

        lax.fori_loop(1, N_LEAF, send_r, 0)
        made = mm(v_wide, tiles[NEAR + 1])
        return backs, made[:8] + made[8:]

    def pass_charges(t):
        sem = it_sem.at[t]
        many = msg_q.at[t, pl.ds(0, N_LEAF - 1)]
        pltpu.make_async_copy(many, many, sem.at[1]).wait()
        extra = jnp.sum(msg_q[t].astype(F32), 0)
        charge = jnp.concatenate([extra[0:1] + extra[2:3], extra[1:2] + extra[3:4]], 1)
        row = iota((8, 128), 0)
        tile = jnp.where(row == 0, charge[:, :128], 0.0)
        tile = jnp.where(row == 1, charge[:, 128:], tile)
        tile = jnp.where(row == 2, extra[6:7] + extra[7:8] + extra[8:9], tile)
        grp_q[t, grp] = tile

        def send_q(j, _):
            pltpu.make_async_remote_copy(
                src_ref=grp_q.at[t, grp], dst_ref=grp_q.at[t, grp], send_sem=sem.at[4], recv_sem=sem.at[5],
                device_id=(grp_peer(j), me), device_id_type=MESH,
            ).start()
            return 0

        lax.fori_loop(1, N_GRP, send_q, 0)
        return charge, extra

    def finish(t, v, terms, group, n_dots, last):
        sem = it_sem.at[t]
        backs, self_part = terms
        charge, extra = group
        lane = iota((8, 128), 1)
        counts = jnp.broadcast_to(jnp.concatenate([extra[4:5], extra[5:6]], 1), (8, BLK))
        mine = iota((8, BLK), 1) == me * OWN + iota((8, BLK), 0)
        weight = own_uses + jnp.sum(jnp.where(mine, counts, 0.0), 1, keepdims=True)
        self_part = weight * self_part
        many = msg_v.at[t, pl.ds(0, N_LEAF - 1)]
        pltpu.make_async_copy(many, many, sem.at[11]).wait()
        vectors = msg_v[t].reshape(N_LEAF * 16, 128)
        found = mm(pick[...].astype(BF16), vectors)
        partners = [
            jnp.concatenate([found[k * 8 : k * 8 + 8], found[(NEAR + k) * 8 : (NEAR + k) * 8 + 8]], 1) for k in range(NEAR)
        ]
        if last:
            share = v * (self_part + noise * v)
            for k in range(NEAR):
                share = share + 2.0 * backs[k] * partners[k]
            quad[me] = sum_all(share)[:1]

            def send_s(j, _):
                pltpu.make_async_remote_copy(
                    src_ref=quad.at[me], dst_ref=quad.at[me], send_sem=sem.at[6], recv_sem=sem.at[7],
                    device_id=(grp, leaf_peer(j)), device_id_type=MESH,
                ).start()
                return 0

            lax.fori_loop(1, N_LEAF, send_s, 0)

        forward = jnp.zeros((16, ROWS_DEV), F32)
        for k in range(NEAR):
            forward = forward + mm_t(jnp.concatenate([partners[k], zero], 0).astype(BF16), tiles[k])
        near = self_part + own_part(forward)
        many = ret_recv.at[t, pl.ds(0, N_LEAF - 1)]
        pltpu.make_async_copy(many, many, sem.at[3]).wait()
        near = near + halves(jnp.sum(ret_recv[t].astype(F32), 0)) + noise * v

        many = grp_q.at[t, pl.ds(0, N_GRP - 1)]
        pltpu.make_async_copy(many, many, sem.at[5]).wait()
        row = iota((8, BLK), 0)
        charges = zero
        sums = jnp.zeros((8, 128), F32)
        for g in range(N_GRP):
            tile = grp_q[t, g]
            charges = jnp.where(row == g, jnp.concatenate([tile[0:1], tile[1:2]], 1), charges)
            sums = sums + tile
        totals = [
            jnp.broadcast_to(jnp.sum(jnp.where(lane[:1] == index, sums[2:3], 0.0), 1, keepdims=True), (8, 128))
            for index in range(n_dots)
        ]
        field = jnp.sum(mm(spread(charges), coup[...]), 0, keepdims=True)
        if last:
            far_share = sum_all(jnp.where(row == 0, charge * field, 0.0))
            many = quad.at[pl.ds(0, N_LEAF - 1)]
            pltpu.make_async_copy(many, many, sem.at[7]).wait()
            grp_s[grp] = jnp.sum(quad[...], 0) + far_share[:1]

            def send_c(j, _):
                pltpu.make_async_remote_copy(
                    src_ref=grp_s.at[grp], dst_ref=grp_s.at[grp], send_sem=sem.at[8], recv_sem=sem.at[9],
                    device_id=(grp_peer(j), me), device_id_type=MESH,
                ).start()
                return 0

            lax.fori_loop(1, N_GRP, send_c, 0)
        far = own_part(mm_t(rows16(jnp.broadcast_to(field, (8, BLK))), tiles[NEAR]))
        quadratic = None
        if last:
            many = grp_s.at[pl.ds(0, N_GRP - 1)]
            pltpu.make_async_copy(many, many, sem.at[9]).wait()
            quadratic = jnp.broadcast_to(jnp.sum(grp_s[...], 0), (8, 128))
        waits = [
            (0, msg_q.at[t, pl.ds(0, N_LEAF - 1)]),
            (10, msg_v.at[t, pl.ds(0, N_LEAF - 1)]),
            (2, ret_recv.at[t, pl.ds(0, N_LEAF - 1)]),
            (4, grp_q.at[t, pl.ds(0, N_GRP - 1)]),
        ]
        if last:
            waits += [(6, quad.at[pl.ds(0, N_LEAF - 1)]), (8, grp_s.at[pl.ds(0, N_GRP - 1)])]
        for index, sent in waits:
            pltpu.make_async_copy(sent, sent, sem.at[index]).wait()
        return near + far, totals, quadratic

    def apply(t, v, dots, last):
        v_wide = send_vector(t, v, dots)
        terms = send_returns(t, v_wide)
        return finish(t, v, terms, pass_charges(t), len(dots), last)

    lax.fori_loop(0, OWN, own_row, 0)
    for half in range(2):
        left, right = at(half, -1, 0), at(half, 1, 0)
        arrived(half, 0, piece(left, half))
        start(hop(half, 2, piece(left, half, 0), right))
        arrived(half, 1, piece(right, half))
        start(hop(half, 3, piece(right, half, 1), left))
    for half in range(2):
        second_axis(half, 1)
        second_axis(half, 2)
    sum_parts()
    for p in range(4):
        if p == 0:
            for half in range(2):
                far = at(half, 2, 0)
                arrived(half, 2, piece(far, half, 0))
                arrived(half, 3, piece(far, half, 1))
                second_axis(half, 3)
        if p == 1:
            send_skeleton()
        for half in range(2):
            down, up = at(half, offsets[p], -1), at(half, offsets[p], 1)
            arrived(half, 4 + 4 * p, piece(down, half))
            start(hop(half, 6 + 4 * p, piece(down, half, 0), at(half, 0, 1)))
            started.append(to_sibling(half, 4 * p + 1, down))
            arrived(half, 5 + 4 * p, piece(up, half))
            start(hop(half, 7 + 4 * p, piece(up, half, 1), at(half, 0, -1)))
            started.append(to_sibling(half, 4 * p + 2, up))
        if p == 2:
            skel_t = make_basis()
    for p in range(4):
        if p == 3:
            make_couplings(skel_t)
        for half in range(2):
            over = at(half, offsets[p], 2)
            arrived(half, 6 + 4 * p, piece(over, half, 0))
            arrived(half, 7 + 4 * p, piece(over, half, 1))
            started.append(to_sibling(half, 4 * p + 3, over))
    first = target * precond
    first_wide = send_vector(0, first, ())
    steps = (0, -1, 1, 2)
    for p in range(4):
        for half in range(2):
            for s in range(4):
                theirs = at(half, offsets[p], steps[s]) - core + lax.rem(core + 1, 2)
                ref = piece(theirs, half)
                pltpu.make_async_remote_copy(
                    src_ref=ref, dst_ref=ref, send_sem=s_send.at[half, 4 * p + s], recv_sem=s_recv.at[half, 4 * p + s],
                    device_id=(grp, sibling), device_id_type=MESH,
                ).wait_recv()
    for copy in started:
        copy.wait_send()

    def tile_row(n, _):
        feat_t = features(jnp.concatenate([grp_cfg[nb_s[n, k]] for k in range(NEAR)], 1))
        made = kernel_of(mm(own_feat[n], feat_t)).astype(BF16)
        for k in range(NEAR):
            tiles[k, pl.ds(n * BLK, BLK), :] = made[:, k * BLK : (k + 1) * BLK]
        return 0

    lax.fori_loop(0, OWN, tile_row, 0)
    first_group = pass_charges(0)

    for index, sent in (
        (0, part_recv.at[pl.ds(0, N_LEAF - 1)]),
        (2, skel_tiles.at[pl.ds(0, N_LEAF // 2 - 1)]),
        (4, skel_cfg.at[pl.ds(0, N_GRP - 1)]),
    ):
        pltpu.make_async_copy(sent, sent, k_sem.at[index]).wait()

    w, _, _ = finish(0, first, send_returns(0, first_wide), first_group, 0, False)

    def step(t, carry):
        x, r, p, s, z, w, gamma_old, energy_old = carry
        u = r * precond
        made, (gamma, delta, mixed), _ = apply(t, w * precond, (r * u, u * w, u * s), False)
        beta = jnp.where(t == 1, jnp.zeros_like(gamma), gamma / gamma_old)
        energy = delta + 2.0 * beta * mixed + beta * beta * energy_old
        alpha = wide(gamma / energy)
        beta = wide(beta)
        p = u + beta * p
        s = w + beta * s
        z = made + beta * z
        return x + alpha * p, r - alpha * s, p, s, z, w - alpha * z, gamma, energy

    x, r, p, s, z, w, gamma_old, energy_old = lax.fori_loop(
        1, ITERS - 1, step, (zero, target, zero, zero, zero, w, one, one)
    )
    u, m, q = r * precond, w * precond, s * precond
    made, sums, m_am = apply(
        ITERS - 1, m, (r * u, u * w, u * s, u * z, m * w, m * z, q * w, q * z, q * s), True
    )
    gamma, delta, mixed, uz, mw, mz, qw, qz, qs = sums
    beta = gamma / gamma_old
    energy = delta + 2.0 * beta * mixed + beta * beta * energy_old
    alpha = gamma / energy
    ss = mw + beta * (2.0 * qw + beta * qs)
    ru = delta + beta * mixed
    gamma_last = gamma - alpha * (2.0 * ru - alpha * ss)
    delta_last = delta - alpha * (2.0 * mw + beta * (uz + qw) - alpha * (m_am + beta * (2.0 * mz + beta * qz)))
    beta_last = gamma_last / gamma
    energy_last = delta_last + beta_last * (2.0 * (ru - alpha * ss) + beta_last * energy)
    alpha_last, alpha, beta, beta_last = (wide(a) for a in (gamma_last / energy_last, alpha, beta, beta_last))
    p = u + beta * p
    s = w + beta * s
    z = made + beta * z
    w = w - alpha * z
    x = x + alpha * p
    r = r - alpha * s
    p = r * precond + beta_last * p
    s = w + beta_last * s
    x = x + alpha_last * p
    r = r - alpha_last * s
    for base, values in ((0, x), (16, r)):
        xr_out[pl.ds(base, 8, stride=2), :] = values[:, :128]
        xr_out[pl.ds(base + 1, 8, stride=2), :] = values[:, 128:]


def on_device(
    configs, order, w_in, bias_in, w_out, noise, right_side, near_blocks, near_live, skeleton
):
    vmem = pl.BlockSpec(memory_space=pltpu.VMEM)
    smem = pl.BlockSpec(memory_space=pltpu.SMEM)
    dma = pltpu.SemaphoreType.DMA
    both = pl.pallas_call(
        body,
        out_shape=jax.ShapeDtypeStruct((32, 128), F32),
        in_specs=[vmem] * 10 + [smem],
        out_specs=vmem,
        scratch_shapes=[
            pltpu.VMEM((N_LEAF * OWN, 64, BLK), BF16),
            pltpu.VMEM((NEAR + 2, ROWS_DEV, BLK), BF16),
            pltpu.VMEM((N_GRP * BLK, BLK), BF16),
            pltpu.VMEM((OWN, BLK, 128), BF16),
            pltpu.VMEM((16, 8, 128), F32),
            pltpu.VMEM((N_LEAF, 8, 128), F32),
            pltpu.VMEM((16, 8, 128), F32),
            pltpu.VMEM((N_GRP, 64, BLK), BF16),
            pltpu.VMEM((128, 512), F32),
            pltpu.VMEM((512, 128), BF16),
            pltpu.VMEM((ITERS, N_LEAF, 16, 128), BF16),
            pltpu.VMEM((ITERS, N_LEAF, 16, 128), BF16),
            pltpu.VMEM((ITERS, N_LEAF, 16, 128), BF16),
            pltpu.VMEM((ITERS, N_LEAF, 16, 128), BF16),
            pltpu.VMEM((N_LEAF, 1, 128), F32),
            pltpu.VMEM((ITERS, N_GRP, 8, 128), F32),
            pltpu.VMEM((N_GRP, 1, 128), F32),
            dma((2, 20)),
            dma((2, 20)),
            dma((2, 16)),
            dma((2, 16)),
            dma((6,)),
            dma((ITERS, 12)),
        ],
        compiler_params=pltpu.CompilerParams(
            collective_id=0, has_side_effects=True, vmem_limit_bytes=56 * 2**20
        ),
        cost_estimate=pl.CostEstimate(flops=10**10, bytes_accessed=10**7, transcendentals=10**7),
    )(
        configs.T, order, w_in, bias_in.reshape(1, 128), w_out,
        noise.reshape(16, 128), right_side.reshape(16, 128), near_blocks, near_live, skeleton, near_blocks,
    )
    return both[:16].reshape(-1), both[16:].reshape(-1)


def solution(mesh):
    in_specs = (
        P(("grp", "leaf"), None),
        P(("grp", "leaf"), None),
        P(),
        P(),
        P(),
        P(("grp", "leaf")),
        P(("grp", "leaf")),
        P(("grp", "leaf"), None),
        P(("grp", "leaf"), None),
        P("grp", None),
    )
    out_specs = (P(("grp", "leaf")), P(("grp", "leaf")))
    return jax.shard_map(
        on_device, mesh=mesh, in_specs=in_specs, out_specs=out_specs, check_vma=False
    )
```

```python
import jax
import jax.numpy as jnp
from jax import lax
from jax.experimental import pallas as pl
from jax.experimental.pallas import tpu as pltpu
from jax.sharding import PartitionSpec as P

BLK = 256
NEAR = 6
ITERS = 4
N_GRP = 8
N_LEAF = 32
OWN = 8
ROWS_DEV = OWN * BLK
F32 = jnp.float32
BF16 = jnp.bfloat16
MESH = pl.DeviceIdType.MESH
SHARP = 10.0 * 1.4426950408889634


def mm(left, right):
    return lax.dot_general(left, right, (((1,), (0,)), ((), ())), preferred_element_type=F32)


def mm_t(left, right):
    return lax.dot_general(left, right, (((1,), (1,)), ((), ())), preferred_element_type=F32)


def iota(shape, dim):
    return lax.broadcasted_iota(jnp.int32, shape, dim)


def kernel_of(inner):
    return jnp.exp2(inner * SHARP - SHARP)


def one_hot(row, base):
    hit = jnp.broadcast_to(row, (BLK, BLK)) == iota((BLK, BLK), 0) + base
    return jnp.where(hit, 1.0, 0.0).astype(BF16)


def flip(values):
    return jnp.transpose(values.astype(F32)).astype(BF16)


def split2(values):
    high = values.astype(BF16).astype(F32)
    return high, (values - high).astype(BF16).astype(F32)


def rows16(values):
    return jnp.concatenate(split2(values), 0).astype(BF16)


def spread(values):
    wide = jnp.concatenate([jnp.concatenate(split2(values), 0)] * OWN, 1)
    shape = (16, ROWS_DEV)
    keep = (iota(shape, 0) & 7) == (iota(shape, 1) >> 8)
    return jnp.where(keep, wide, 0.0).astype(BF16)


def own_part(wide):
    both = wide[:8] + wide[8:]
    row = iota((8, BLK), 0)
    total = jnp.zeros((8, BLK), F32)
    for n in range(OWN):
        total = total + jnp.where(row == n, both[:, n * BLK : (n + 1) * BLK], 0.0)
    return total


def halves(values):
    return jnp.concatenate([values[:8], values[8:]], 1)


def sum_all(values):
    folded = values[:, :128] + values[:, 128:]
    return jnp.broadcast_to(jnp.sum(folded, (0, 1), keepdims=True), (8, 128))


def wide(values):
    return jnp.concatenate([values, values], 1)


def column_of(row):
    return jnp.transpose(jnp.broadcast_to(row.astype(F32), (128, 128)))


def body(
    cfg_ref, order_ref, w_in_ref, bias_ref, w_out_ref, noise_ref, rhs_ref, nb_ref, live_ref, skel_ref,
    nb_s,
    xr_out,
    grp_cfg, tiles, coup, own_feat, part_send, part_recv, skel_tiles, skel_cfg, pick, pick_t,
    msg_q, msg_v, ret_send, ret_recv, quad, grp_q, grp_s,
    g_send, g_recv, s_send, s_recv, k_sem, it_sem,
):
    grp = lax.axis_index("grp")
    me = lax.axis_index("leaf")
    core = lax.rem(me, 2)
    xx = lax.rem(me // 2, 4)
    yy = me // 8

    def leaf_at(y, x, c):
        return lax.rem(y + 4, 4) * 8 + lax.rem(x + 4, 4) * 2 + c

    def leaf_peer(j):
        return lax.rem(me + j, N_LEAF)

    def grp_peer(j):
        return lax.rem(grp + j, N_GRP)

    barrier = pltpu.get_barrier_semaphore()

    def greet_leaf(j, _):
        pl.semaphore_signal(barrier, inc=1, device_id=(grp, leaf_peer(j)), device_id_type=MESH)
        return 0

    def greet_grp(j, _):
        pl.semaphore_signal(barrier, inc=1, device_id=(grp_peer(j), me), device_id_type=MESH)
        return 0

    lax.fori_loop(1, N_LEAF, greet_leaf, 0)
    lax.fori_loop(1, N_GRP, greet_grp, 0)

    def permute(b, _):
        row = order_ref[:, pl.ds(pl.multiple_of(b * BLK, BLK), BLK)]
        total = jnp.zeros((64, BLK), F32)
        for c in range(OWN):
            total = total + mm(cfg_ref[:, c * BLK : (c + 1) * BLK], one_hot(row, c * BLK))
        grp_cfg[me * OWN + b] = total.astype(BF16)
        return 0

    def at(half, first, second):
        return leaf_at(yy + second, xx + first, core) if half == 0 else leaf_at(yy + first, xx + second, core)

    def piece(leaf, half, quarter=None):
        if quarter is None:
            return grp_cfg.at[pl.ds(leaf * OWN + 4 * half, 4)]
        return grp_cfg.at[pl.ds(leaf * OWN + 4 * half + 2 * quarter, 2)]

    def hop(half, index, ref, target):
        return pltpu.make_async_remote_copy(
            src_ref=ref, dst_ref=ref, send_sem=g_send.at[half, index], recv_sem=g_recv.at[half, index],
            device_id=(grp, target), device_id_type=MESH,
        )

    sibling = me - core + lax.rem(core + 1, 2)

    def to_sibling(half, index, leaf):
        ref = piece(leaf, half)
        copy = pltpu.make_async_remote_copy(
            src_ref=ref, dst_ref=ref, send_sem=s_send.at[half, index], recv_sem=s_recv.at[half, index],
            device_id=(grp, sibling), device_id_type=MESH,
        )
        copy.start()
        return copy

    started = []

    def start(copy):
        copy.start()
        started.append(copy)

    offsets = (0, -1, 1, 2)

    def second_axis(half, p):
        ref = piece(at(half, offsets[p], 0), half)
        start(hop(half, 4 + 4 * p, ref, at(half, 0, 1)))
        start(hop(half, 5 + 4 * p, ref, at(half, 0, -1)))
        started.append(to_sibling(half, 4 * p, at(half, offsets[p], 0)))

    def arrived(half, index, ref):
        hop(half, index, ref, me).wait_recv()

    for half in range(2):
        lax.fori_loop(4 * half, 4 * half + 4, permute, 0)
        if half == 0:
            pl.semaphore_wait(barrier, N_LEAF - 1 + N_GRP - 1)
        own = piece(me, half)
        start(hop(half, 0, own, at(half, 1, 0)))
        start(hop(half, 1, own, at(half, -1, 0)))

    def choose(b, total):
        return total + mm(grp_cfg[me * OWN + b], one_hot(skel_ref[...] - me * ROWS_DEV, b * BLK))

    given = lax.fori_loop(0, OWN, choose, jnp.zeros((64, BLK), F32))
    for q in range(16):
        part_send[q] = given[q // 2 * 8 : q // 2 * 8 + 8, q % 2 * 128 : q % 2 * 128 + 128]
    part_recv[me] = part_send[me // 2]

    def send_part(j, _):
        peer = leaf_peer(j)
        pltpu.make_async_remote_copy(
            src_ref=part_send.at[peer // 2], dst_ref=part_recv.at[me], send_sem=k_sem.at[0], recv_sem=k_sem.at[1],
            device_id=(grp, peer), device_id_type=MESH,
        ).start()
        return 0

    lax.fori_loop(1, N_LEAF, send_part, 0)
    for half in range(2):
        second_axis(half, 0)

    w_in_t = flip(w_in_ref[...])
    w_out_t = flip(w_out_ref[...])
    bias = column_of(bias_ref[...])

    def features(configs):
        hidden = mm(w_in_t, configs)
        hidden = jnp.tanh(hidden + jnp.concatenate([bias] * (configs.shape[1] // 128), 1)).astype(BF16)
        raw = mm(w_out_t, hidden)
        return (raw * lax.rsqrt(jnp.sum(raw * raw, 0, keepdims=True) + 1e-06)).astype(BF16)

    def own_row(n, _):
        feat_t = features(grp_cfg[me * OWN + n])
        feat = flip(feat_t)
        own_feat[n] = feat
        tiles[NEAR + 1, pl.ds(n * BLK, BLK), :] = kernel_of(mm(feat, feat_t)).astype(BF16)
        return 0

    def sum_parts():
        many = part_recv.at[pl.ds(0, N_LEAF - 1)]
        pltpu.make_async_copy(many, many, k_sem.at[1]).wait()
        skel_tiles[me // 2] = jnp.sum(part_recv[...], 0)

        def send_tile(j, _):
            pltpu.make_async_remote_copy(
                src_ref=skel_tiles.at[me // 2], dst_ref=skel_tiles.at[me // 2], send_sem=k_sem.at[2], recv_sem=k_sem.at[3],
                device_id=(grp, leaf_peer(2 * j)), device_id_type=MESH,
            ).start()
            return 0

        lax.fori_loop(1, N_LEAF // 2, send_tile, 0)

    def send_skeleton():
        many = skel_tiles.at[pl.ds(0, N_LEAF // 2 - 1)]
        pltpu.make_async_copy(many, many, k_sem.at[3]).wait()
        for h in range(2):
            skel_cfg[grp, :, h * 128 : (h + 1) * 128] = jnp.concatenate(
                [skel_tiles[2 * q + h] for q in range(8)], 0
            ).astype(BF16)

        def send_skel(j, _):
            pltpu.make_async_remote_copy(
                src_ref=skel_cfg.at[grp], dst_ref=skel_cfg.at[grp], send_sem=k_sem.at[4], recv_sem=k_sem.at[5],
                device_id=(grp_peer(j), me), device_id_type=MESH,
            ).start()
            return 0

        lax.fori_loop(1, N_GRP, send_skel, 0)

    def make_basis():
        skel_t = features(skel_cfg[grp])

        def basis(n, _):
            tiles[NEAR, pl.ds(n * BLK, BLK), :] = kernel_of(mm(own_feat[n], skel_t)).astype(BF16)
            return 0

        lax.fori_loop(0, OWN, basis, 0)
        return skel_t

    def make_couplings(skel_t):
        many = skel_cfg.at[pl.ds(0, N_GRP - 1)]
        pltpu.make_async_copy(many, many, k_sem.at[5]).wait()

        def couple(g, _):
            coup[pl.ds(g * BLK, BLK), :] = kernel_of(mm(flip(features(skel_cfg[g])), skel_t)).astype(BF16)
            return 0

        lax.fori_loop(0, N_GRP, couple, 0)

    nb = nb_ref[...]
    live = live_ref[...].astype(F32)
    place = nb + (nb & -8)
    for h in range(2):
        for k in range(NEAR):
            hit = iota((8, 512), 1) == place[:, k : k + 1] + 8 * h
            pick[pl.ds((h * NEAR + k) * 8, 8), :] = jnp.where(hit, live[:, k : k + 1], 0.0)
    pick[pl.ds(96, 32), :] = jnp.zeros((32, 512), F32)
    for q in range(4):
        pick_t[pl.ds(q * 128, 128), :] = jnp.transpose(pick[:, q * 128 : (q + 1) * 128]).astype(BF16)
    count = jnp.zeros((8, BLK), F32)
    for k in range(NEAR):
        count = count + jnp.where(iota((8, BLK), 1) == nb[:, k : k + 1], live[:, k : k + 1], 0.0)
    count = jnp.sum(count, 0, keepdims=True)
    own_uses = jnp.sum(live, 1, keepdims=True)

    noise = jnp.concatenate([noise_ref[pl.ds(0, 8, stride=2), :], noise_ref[pl.ds(1, 8, stride=2), :]], 1)
    target = jnp.concatenate([rhs_ref[pl.ds(0, 8, stride=2), :], rhs_ref[pl.ds(1, 8, stride=2), :]], 1)
    precond = 1.0 / (1.0 + noise)
    zero = jnp.zeros((8, BLK), F32)
    one = jnp.ones((8, 128), F32)

    def send_vector(t, v, dots):
        sem = it_sem.at[t]
        v_wide = spread(v)
        charge = jnp.sum(mm(v_wide, tiles[NEAR]), 0, keepdims=True)

        c_high, c_mid = split2(charge)
        rows = [c_high[:, :128], c_high[:, 128:], c_mid[:, :128], c_mid[:, 128:], count[:, :128], count[:, 128:]]
        lane = iota((8, 128), 1)
        sums = jnp.zeros((8, 128), F32)
        for index, values in enumerate(dots):
            sums = jnp.where(lane == index, sum_all(values), sums)
        s_high, s_mid = split2(sums)
        rows += [s_high[:1], s_mid[:1], (sums - s_high - s_mid)[:1]]
        row = iota((16, 128), 0)
        extra = jnp.zeros((16, 128), F32)
        for at_row, values in enumerate(rows):
            extra = jnp.where(row == at_row, values, extra)
        msg_q[t, me] = extra.astype(BF16)
        msg_v[t, me] = jnp.concatenate([v[:, :128], v[:, 128:]], 0).astype(BF16)
        for ref, index in ((msg_q, 0), (msg_v, 10)):

            def send_a(j, _, ref=ref, index=index):
                pltpu.make_async_remote_copy(
                    src_ref=ref.at[t, me], dst_ref=ref.at[t, me], send_sem=sem.at[index], recv_sem=sem.at[index + 1],
                    device_id=(grp, leaf_peer(j)), device_id_type=MESH,
                ).start()
                return 0

            lax.fori_loop(1, N_LEAF, send_a, 0)
        return v_wide

    def send_returns(t, v_wide):
        sem = it_sem.at[t]
        backs = []
        for k in range(NEAR):
            made = mm(v_wide, tiles[k])
            backs.append(made[:8] + made[8:])
        stack = jnp.concatenate([b[:, :128] for b in backs] + [b[:, 128:] for b in backs] + [jnp.zeros((32, 128), F32)], 0)
        b_high, b_mid = split2(stack)
        returned = mm(pick_t[...], b_high.astype(BF16)) + mm(pick_t[...], b_mid.astype(BF16))
        ret_send[t] = returned.reshape(N_LEAF, 16, 128).astype(BF16)
        ret_recv[t, me] = ret_send[t, me]

        def send_r(j, _):
            peer = leaf_peer(j)
            pltpu.make_async_remote_copy(
                src_ref=ret_send.at[t, peer], dst_ref=ret_recv.at[t, me], send_sem=sem.at[2], recv_sem=sem.at[3],
                device_id=(grp, peer), device_id_type=MESH,
            ).start()
            return 0

        lax.fori_loop(1, N_LEAF, send_r, 0)
        made = mm(v_wide, tiles[NEAR + 1])
        return backs, made[:8] + made[8:]

    def pass_charges(t):
        sem = it_sem.at[t]
        many = msg_q.at[t, pl.ds(0, N_LEAF - 1)]
        pltpu.make_async_copy(many, many, sem.at[1]).wait()
        extra = jnp.sum(msg_q[t].astype(F32), 0)
        charge = jnp.concatenate([extra[0:1] + extra[2:3], extra[1:2] + extra[3:4]], 1)
        row = iota((8, 128), 0)
        tile = jnp.where(row == 0, charge[:, :128], 0.0)
        tile = jnp.where(row == 1, charge[:, 128:], tile)
        tile = jnp.where(row == 2, extra[6:7] + extra[7:8] + extra[8:9], tile)
        grp_q[t, grp] = tile

        def send_q(j, _):
            pltpu.make_async_remote_copy(
                src_ref=grp_q.at[t, grp], dst_ref=grp_q.at[t, grp], send_sem=sem.at[4], recv_sem=sem.at[5],
                device_id=(grp_peer(j), me), device_id_type=MESH,
            ).start()
            return 0

        lax.fori_loop(1, N_GRP, send_q, 0)
        return charge, extra

    def finish(t, v, terms, group, n_dots, last):
        sem = it_sem.at[t]
        backs, self_part = terms
        charge, extra = group
        lane = iota((8, 128), 1)
        counts = jnp.broadcast_to(jnp.concatenate([extra[4:5], extra[5:6]], 1), (8, BLK))
        mine = iota((8, BLK), 1) == me * OWN + iota((8, BLK), 0)
        weight = own_uses + jnp.sum(jnp.where(mine, counts, 0.0), 1, keepdims=True)
        self_part = weight * self_part
        many = msg_v.at[t, pl.ds(0, N_LEAF - 1)]
        pltpu.make_async_copy(many, many, sem.at[11]).wait()
        vectors = msg_v[t].reshape(N_LEAF * 16, 128)
        found = mm(pick[...].astype(BF16), vectors)
        partners = [
            jnp.concatenate([found[k * 8 : k * 8 + 8], found[(NEAR + k) * 8 : (NEAR + k) * 8 + 8]], 1) for k in range(NEAR)
        ]
        if last:
            share = v * (self_part + noise * v)
            for k in range(NEAR):
                share = share + 2.0 * backs[k] * partners[k]
            quad[me] = sum_all(share)[:1]

            def send_s(j, _):
                pltpu.make_async_remote_copy(
                    src_ref=quad.at[me], dst_ref=quad.at[me], send_sem=sem.at[6], recv_sem=sem.at[7],
                    device_id=(grp, leaf_peer(j)), device_id_type=MESH,
                ).start()
                return 0

            lax.fori_loop(1, N_LEAF, send_s, 0)

        forward = jnp.zeros((16, ROWS_DEV), F32)
        for k in range(NEAR):
            forward = forward + mm_t(jnp.concatenate([partners[k], zero], 0).astype(BF16), tiles[k])
        near = self_part + own_part(forward)
        many = ret_recv.at[t, pl.ds(0, N_LEAF - 1)]
        pltpu.make_async_copy(many, many, sem.at[3]).wait()
        near = near + halves(jnp.sum(ret_recv[t].astype(F32), 0)) + noise * v

        many = grp_q.at[t, pl.ds(0, N_GRP - 1)]
        pltpu.make_async_copy(many, many, sem.at[5]).wait()
        row = iota((8, BLK), 0)
        charges = zero
        sums = jnp.zeros((8, 128), F32)
        for g in range(N_GRP):
            tile = grp_q[t, g]
            charges = jnp.where(row == g, jnp.concatenate([tile[0:1], tile[1:2]], 1), charges)
            sums = sums + tile
        totals = [
            jnp.broadcast_to(jnp.sum(jnp.where(lane[:1] == index, sums[2:3], 0.0), 1, keepdims=True), (8, 128))
            for index in range(n_dots)
        ]
        field = jnp.sum(mm(spread(charges), coup[...]), 0, keepdims=True)
        if last:
            far_share = sum_all(jnp.where(row == 0, charge * field, 0.0))
            many = quad.at[pl.ds(0, N_LEAF - 1)]
            pltpu.make_async_copy(many, many, sem.at[7]).wait()
            grp_s[grp] = jnp.sum(quad[...], 0) + far_share[:1]

            def send_c(j, _):
                pltpu.make_async_remote_copy(
                    src_ref=grp_s.at[grp], dst_ref=grp_s.at[grp], send_sem=sem.at[8], recv_sem=sem.at[9],
                    device_id=(grp_peer(j), me), device_id_type=MESH,
                ).start()
                return 0

            lax.fori_loop(1, N_GRP, send_c, 0)
        far = own_part(mm_t(rows16(jnp.broadcast_to(field, (8, BLK))), tiles[NEAR]))
        quadratic = None
        if last:
            many = grp_s.at[pl.ds(0, N_GRP - 1)]
            pltpu.make_async_copy(many, many, sem.at[9]).wait()
            quadratic = jnp.broadcast_to(jnp.sum(grp_s[...], 0), (8, 128))
        waits = [
            (0, msg_q.at[t, pl.ds(0, N_LEAF - 1)]),
            (10, msg_v.at[t, pl.ds(0, N_LEAF - 1)]),
            (2, ret_recv.at[t, pl.ds(0, N_LEAF - 1)]),
            (4, grp_q.at[t, pl.ds(0, N_GRP - 1)]),
        ]
        if last:
            waits += [(6, quad.at[pl.ds(0, N_LEAF - 1)]), (8, grp_s.at[pl.ds(0, N_GRP - 1)])]
        for index, sent in waits:
            pltpu.make_async_copy(sent, sent, sem.at[index]).wait()
        return near + far, totals, quadratic

    def apply(t, v, dots, last):
        v_wide = send_vector(t, v, dots)
        terms = send_returns(t, v_wide)
        return finish(t, v, terms, pass_charges(t), len(dots), last)

    lax.fori_loop(0, OWN, own_row, 0)
    for half in range(2):
        left, right = at(half, -1, 0), at(half, 1, 0)
        arrived(half, 0, piece(left, half))
        start(hop(half, 2, piece(left, half, 0), right))
        arrived(half, 1, piece(right, half))
        start(hop(half, 3, piece(right, half, 1), left))
    for half in range(2):
        second_axis(half, 1)
        second_axis(half, 2)
    sum_parts()
    for p in range(4):
        if p == 0:
            for half in range(2):
                far = at(half, 2, 0)
                arrived(half, 2, piece(far, half, 0))
                arrived(half, 3, piece(far, half, 1))
                second_axis(half, 3)
        if p == 1:
            send_skeleton()
        for half in range(2):
            down, up = at(half, offsets[p], -1), at(half, offsets[p], 1)
            arrived(half, 4 + 4 * p, piece(down, half))
            start(hop(half, 6 + 4 * p, piece(down, half, 0), at(half, 0, 1)))
            started.append(to_sibling(half, 4 * p + 1, down))
            arrived(half, 5 + 4 * p, piece(up, half))
            start(hop(half, 7 + 4 * p, piece(up, half, 1), at(half, 0, -1)))
            started.append(to_sibling(half, 4 * p + 2, up))
        if p == 2:
            skel_t = make_basis()
    for p in range(4):
        for half in range(2):
            over = at(half, offsets[p], 2)
            arrived(half, 6 + 4 * p, piece(over, half, 0))
            arrived(half, 7 + 4 * p, piece(over, half, 1))
            started.append(to_sibling(half, 4 * p + 3, over))
    first = target * precond
    first_wide = send_vector(0, first, ())
    steps = (0, -1, 1, 2)
    for p in range(4):
        for half in range(2):
            for s in range(4):
                theirs = at(half, offsets[p], steps[s]) - core + lax.rem(core + 1, 2)
                ref = piece(theirs, half)
                pltpu.make_async_remote_copy(
                    src_ref=ref, dst_ref=ref, send_sem=s_send.at[half, 4 * p + s], recv_sem=s_recv.at[half, 4 * p + s],
                    device_id=(grp, sibling), device_id_type=MESH,
                ).wait_recv()
    for copy in started:
        copy.wait_send()

    def tile_row(n, _):
        feat_t = features(jnp.concatenate([grp_cfg[nb_s[n, k]] for k in range(NEAR)], 1))
        made = kernel_of(mm(own_feat[n], feat_t)).astype(BF16)
        for k in range(NEAR):
            tiles[k, pl.ds(n * BLK, BLK), :] = made[:, k * BLK : (k + 1) * BLK]
        return 0

    lax.fori_loop(0, OWN, tile_row, 0)
    first_group = pass_charges(0)

    for index, sent in (
        (0, part_recv.at[pl.ds(0, N_LEAF - 1)]),
        (2, skel_tiles.at[pl.ds(0, N_LEAF // 2 - 1)]),
        (4, skel_cfg.at[pl.ds(0, N_GRP - 1)]),
    ):
        pltpu.make_async_copy(sent, sent, k_sem.at[index]).wait()

    first_terms = send_returns(0, first_wide)
    make_couplings(skel_t)
    w, _, _ = finish(0, first, first_terms, first_group, 0, False)

    def step(t, carry):
        x, r, p, s, z, w, gamma_old, energy_old = carry
        u = r * precond
        made, (gamma, delta, mixed), _ = apply(t, w * precond, (r * u, u * w, u * s), False)
        beta = jnp.where(t == 1, jnp.zeros_like(gamma), gamma / gamma_old)
        energy = delta + 2.0 * beta * mixed + beta * beta * energy_old
        alpha = wide(gamma / energy)
        beta = wide(beta)
        p = u + beta * p
        s = w + beta * s
        z = made + beta * z
        return x + alpha * p, r - alpha * s, p, s, z, w - alpha * z, gamma, energy

    x, r, p, s, z, w, gamma_old, energy_old = lax.fori_loop(
        1, ITERS - 1, step, (zero, target, zero, zero, zero, w, one, one)
    )
    u, m, q = r * precond, w * precond, s * precond
    made, sums, m_am = apply(
        ITERS - 1, m, (r * u, u * w, u * s, u * z, m * w, m * z, q * w, q * z, q * s), True
    )
    gamma, delta, mixed, uz, mw, mz, qw, qz, qs = sums
    beta = gamma / gamma_old
    energy = delta + 2.0 * beta * mixed + beta * beta * energy_old
    alpha = gamma / energy
    ss = mw + beta * (2.0 * qw + beta * qs)
    ru = delta + beta * mixed
    gamma_last = gamma - alpha * (2.0 * ru - alpha * ss)
    delta_last = delta - alpha * (2.0 * mw + beta * (uz + qw) - alpha * (m_am + beta * (2.0 * mz + beta * qz)))
    beta_last = gamma_last / gamma
    energy_last = delta_last + beta_last * (2.0 * (ru - alpha * ss) + beta_last * energy)
    alpha_last, alpha, beta, beta_last = (wide(a) for a in (gamma_last / energy_last, alpha, beta, beta_last))
    p = u + beta * p
    s = w + beta * s
    z = made + beta * z
    w = w - alpha * z
    x = x + alpha * p
    r = r - alpha * s
    p = r * precond + beta_last * p
    s = w + beta_last * s
    x = x + alpha_last * p
    r = r - alpha_last * s
    for base, values in ((0, x), (16, r)):
        xr_out[pl.ds(base, 8, stride=2), :] = values[:, :128]
        xr_out[pl.ds(base + 1, 8, stride=2), :] = values[:, 128:]


def on_device(
    configs, order, w_in, bias_in, w_out, noise, right_side, near_blocks, near_live, skeleton
):
    vmem = pl.BlockSpec(memory_space=pltpu.VMEM)
    smem = pl.BlockSpec(memory_space=pltpu.SMEM)
    dma = pltpu.SemaphoreType.DMA
    both = pl.pallas_call(
        body,
        out_shape=jax.ShapeDtypeStruct((32, 128), F32),
        in_specs=[vmem] * 10 + [smem],
        out_specs=vmem,
        scratch_shapes=[
            pltpu.VMEM((N_LEAF * OWN, 64, BLK), BF16),
            pltpu.VMEM((NEAR + 2, ROWS_DEV, BLK), BF16),
            pltpu.VMEM((N_GRP * BLK, BLK), BF16),
            pltpu.VMEM((OWN, BLK, 128), BF16),
            pltpu.VMEM((16, 8, 128), F32),
            pltpu.VMEM((N_LEAF, 8, 128), F32),
            pltpu.VMEM((16, 8, 128), F32),
            pltpu.VMEM((N_GRP, 64, BLK), BF16),
            pltpu.VMEM((128, 512), F32),
            pltpu.VMEM((512, 128), BF16),
            pltpu.VMEM((ITERS, N_LEAF, 16, 128), BF16),
            pltpu.VMEM((ITERS, N_LEAF, 16, 128), BF16),
            pltpu.VMEM((ITERS, N_LEAF, 16, 128), BF16),
            pltpu.VMEM((ITERS, N_LEAF, 16, 128), BF16),
            pltpu.VMEM((N_LEAF, 1, 128), F32),
            pltpu.VMEM((ITERS, N_GRP, 8, 128), F32),
            pltpu.VMEM((N_GRP, 1, 128), F32),
            dma((2, 20)),
            dma((2, 20)),
            dma((2, 16)),
            dma((2, 16)),
            dma((6,)),
            dma((ITERS, 12)),
        ],
        compiler_params=pltpu.CompilerParams(
            collective_id=0, has_side_effects=True, vmem_limit_bytes=56 * 2**20
        ),
        cost_estimate=pl.CostEstimate(flops=10**10, bytes_accessed=10**7, transcendentals=10**7),
    )(
        configs.T, order, w_in, bias_in.reshape(1, 128), w_out,
        noise.reshape(16, 128), right_side.reshape(16, 128), near_blocks, near_live, skeleton, near_blocks,
    )
    return both[:16].reshape(-1), both[16:].reshape(-1)


def solution(mesh):
    in_specs = (
        P(("grp", "leaf"), None),
        P(("grp", "leaf"), None),
        P(),
        P(),
        P(),
        P(("grp", "leaf")),
        P(("grp", "leaf")),
        P(("grp", "leaf"), None),
        P(("grp", "leaf"), None),
        P("grp", None),
    )
    out_specs = (P(("grp", "leaf")), P(("grp", "leaf")))
    return jax.shard_map(
        on_device, mesh=mesh, in_specs=in_specs, out_specs=out_specs, check_vma=False
    )
```
